256 devices in a mesh: ctx: 32 (over z, y), tp: 8 (over x, core).
Axes of the slice: x: 4, y: 4, z: 8, core: 2. Of those that a mesh axis runs over, the one named last changes fastest.
Arguments:
- projected: bfloat16 [3, 8192, 4096], P(None, 'ctx', 'tp'), may hold values from -6 to 6
- short_taps: float32 [3, 7, 4096], P(None, None, 'tp'), may hold values from -2 to 2
- pole_decay: float32 [8, 4096], P(None, 'tp'), as said below
- residues: float32 [8, 4096], P(None, 'tp'), may hold values from -2 to 2
- doc_lengths: int32 [16], replicated, may hold values from 1 to 4096, 8192 in all
- cotangent: bfloat16 [8192, 4096], P('ctx', 'tp'), may hold values from -6 to 6
Outputs:
- gated_out: bfloat16 [8192, 4096], P('ctx', 'tp')
- grad_projected: bfloat16 [3, 8192, 4096], P(None, 'ctx', 'tp')
- grad_taps: float32 [3, 7, 4096], P(None, None, 'tp')
- grad_residues: float32 [8, 4096], P(None, 'tp')
The draws below stay inside these ranges and needn't reach their ends.
Inputs may be any that keep to these rules, and one draw needn't show every extreme that they name: `pole_decay`: each entry lies strictly between 0 and 1. `doc_lengths`: the lengths sum to 8192.
All inputs are finite; a program needn't handle non-finite values.
Results may differ from the reference program's by a relative error of at most 0.023.
Values may be sent and summed in bfloat16 or wider, within the bound.
No kernel may reach another device: no remote copies, remote signals or barrier semaphores. Data moves between devices by JAX's collectives and lax.ppermute only.
A program may use at most 128 MiB of HBM per device.

```python
import math
import jax
import jax.numpy as jnp
import numpy as np
from jax import lax

C = 4096
MODES = 8
TAPS = 7
NDOC = 16
TOKENS = 8192


def draw_pole_decay(key, part):
    key = jax.random.fold_in(key, 11)
    pick_key, fast_key, slow_key = jax.random.split(key, 3)
    fast_share = 0.5
    fast_pick = jax.random.uniform(pick_key, (MODES, C), jnp.float32) < fast_share
    fast_rate = jnp.exp(jax.random.uniform(fast_key, (MODES, C), jnp.float32, math.log(1.0 / 50.0), math.log(1.0 / 30.0)))
    slow_rate = jnp.exp(jax.random.uniform(slow_key, (MODES, C), jnp.float32, math.log(0.1), 0.0)) * (math.log(10.0) / TOKENS)
    return jnp.exp(-jnp.where(fast_pick, fast_rate, slow_rate)).astype(jnp.float32)


def level_of(key, shape, cuts, low, high):
    gain = 1.0
    for dim, parts in cuts:
        steps = jax.random.uniform(jax.random.fold_in(jax.random.fold_in(key, 6), dim), (parts,), jnp.float32, low / len(cuts), high / len(cuts))
        gain = gain * jnp.repeat(jnp.exp(steps), shape[dim] // parts).reshape((-1,) + (1,) * (len(shape) - 1 - dim))
    return gain


def profile(count, total, most, lean):
    portions = [(1 << 20) // math.isqrt(rank ** lean) + 1 for rank in range(2, count + 1)]
    spare, given = total - most - (count - 1), [1] * (count - 1)
    while spare > 0:
        movable = [i for i in range(count - 1) if given[i] < most]
        whole, left = sum([portions[i] for i in movable]), spare
        for i in movable:
            more = min(most - given[i], max(1, left * portions[i] // whole), spare)
            given[i] = given[i] + more
            spare = spare - more
    return np.array([most] + given)


def ragged(own_key, amount, total, reach, lean):
    if amount == 2:
        one = jax.random.randint(own_key, (), max(1, total - reach), min(reach, total - 1) + 1)
        return jnp.stack([one, total - one])
    lengths = jnp.asarray(profile(amount, total, reach, lean), jnp.int32)
    twos = (amount - 1) // 2
    giver, sink = lengths[1:1 + 2 * twos:2], lengths[2:2 + 2 * twos:2]
    room = jnp.minimum(giver - 1, reach - sink)
    moved = jax.random.randint(jax.random.fold_in(own_key, 1), (twos,), 0, 1 << 20) % (room + 1)
    lengths = lengths.at[1:1 + 2 * twos:2].set(giver - moved).at[2:2 + 2 * twos:2].set(sink + moved)
    return lengths[jax.random.permutation(jax.random.fold_in(own_key, 2), amount)]


def noise(stream_key, extent, scale, most, cuts=(), kind=jnp.bfloat16):
    result = scale * jax.random.normal(stream_key, extent, jnp.float32)
    if cuts:
        result = result * level_of(stream_key, extent, cuts, -0.22, 0.18)
    return jnp.clip(result, -most, most).astype(kind)


def setup_inputs(seed: int = 0) -> dict:
    keys = jax.random.split(jax.random.key(seed), 7)
    projected = noise(keys[0], (3, TOKENS, C), 1.0, 6.0, ((1, 32), (2, 8)))
    short_taps = noise(keys[1], (3, TAPS, C), TAPS ** -0.5, 2.0, ((2, 8),), jnp.float32)
    pole_decay = draw_pole_decay(jax.random.fold_in(keys[6], 71), 0)
    residues = noise(keys[3], (MODES, C), 0.35, 2.0, ((1, 8),), jnp.float32)
    doc_lengths = ragged(keys[4], NDOC, TOKENS, TOKENS // 2, 2).astype(jnp.int32)
    cotangent = noise(keys[5], (TOKENS, C), 1.0, 6.0, ((0, 32), (1, 8)))
    return dict(projected=projected, short_taps=short_taps, pole_decay=pole_decay, residues=residues, doc_lengths=doc_lengths, cotangent=cotangent)


def doc_of(positions, doc_lengths):
    end_rows = jnp.cumsum(doc_lengths).astype(jnp.int32)
    counted = lax.optimization_barrier(jnp.sum((positions[:, None] >= end_rows[None, :]).astype(jnp.int32), axis=1))
    return jnp.where(positions < 0, -1, counted).astype(jnp.int32)

def featurize(extended, short_taps, ext_docs):
    tap_span = short_taps.shape[1] - 1
    row_count = extended.shape[1] - tap_span
    own_docs = ext_docs[tap_span:]
    running = jnp.zeros((extended.shape[0], row_count, extended.shape[2]), jnp.float32)
    for tap_lag in range(tap_span + 1):
        same_doc = (ext_docs[tap_span - tap_lag:tap_span - tap_lag + row_count] == own_docs).astype(jnp.float32)
        moved = extended[:, tap_span - tap_lag:tap_span - tap_lag + row_count, :].astype(jnp.float32)
        running = running + short_taps[:, tap_lag, None, :] * moved * same_doc[None, :, None]
    return running

def unfeaturize(extended_grads, short_taps, ext_docs):
    tap_span = short_taps.shape[1] - 1
    row_count = extended_grads.shape[1] - tap_span
    own_docs = ext_docs[:row_count]
    running = jnp.zeros((extended_grads.shape[0], row_count, extended_grads.shape[2]), jnp.float32)
    for tap_lag in range(tap_span + 1):
        same_doc = (ext_docs[tap_lag:tap_lag + row_count] == own_docs).astype(jnp.float32)
        running = running + short_taps[:, tap_lag, None, :] * extended_grads[:, tap_lag:tap_lag + row_count, :] * same_doc[None, :, None]
    return running

def tap_grads(grad_feats, extended, ext_docs):
    tap_span = extended.shape[1] - grad_feats.shape[1]
    row_count = grad_feats.shape[1]
    own_docs = ext_docs[tap_span:]
    pieces = []
    for tap_lag in range(tap_span + 1):
        same_doc = (ext_docs[tap_span - tap_lag:tap_span - tap_lag + row_count] == own_docs).astype(jnp.float32)
        moved = extended[:, tap_span - tap_lag:tap_span - tap_lag + row_count, :].astype(jnp.float32)
        pieces.append(lax.optimization_barrier(jnp.sum(grad_feats * moved * same_doc[None, :, None], axis=1)))
    return jnp.stack(pieces, axis=1)

def compose(earlier, later):
    return (earlier[0] * later[0], earlier[1] * later[0] + later[1])

def stretch_summary(carried, pole_decay, doc_ids, doc_before, block_rows):
    row_count, chan_count = carried.shape
    mode_count = pole_decay.shape[0]
    stretch_count = row_count // block_rows
    offsets = jnp.arange(block_rows, dtype=jnp.float32)
    rising = pole_decay[None] ** offsets[:, None, None]
    falling = pole_decay[None] ** (-offsets[:, None, None])
    weighted = carried.reshape(stretch_count, block_rows, 1, chan_count).astype(jnp.float32) * falling[None]
    stretch_docs = doc_ids.reshape(stretch_count, block_rows)
    shifted = jnp.concatenate([jnp.reshape(doc_before, (1,)).astype(jnp.int32), doc_ids[:-1].astype(jnp.int32)])
    before = shifted[::block_rows]
    lower_mask = offsets[:, None] >= offsets[None, :]
    doc_mask = jnp.logical_and(lower_mask[None], stretch_docs[:, :, None] == stretch_docs[:, None, :]).astype(jnp.float32)
    inner_sums = jnp.einsum('jts,jsx->jtx', doc_mask, weighted.reshape(stretch_count, block_rows, mode_count * chan_count), precision=lax.Precision.HIGHEST)
    inner_sums = inner_sums.reshape(stretch_count, block_rows, mode_count, chan_count)
    keep_mask = (stretch_docs == before[:, None]).astype(jnp.float32)
    end_states = pole_decay ** (block_rows - 1) * inner_sums[:, -1]
    pass_factors = pole_decay ** block_rows * keep_mask[:, -1, None, None]
    factors, states = lax.associative_scan(compose, (pass_factors, end_states), axis=0)
    return (inner_sums, keep_mask, rising, factors, states)

def finish(summary, pole_decay, carry_in):
    inner_sums, keep_mask, rising, factors, states = summary
    prior_state = jnp.concatenate([carry_in[None], states[:-1] + factors[:-1] * carry_in[None]], axis=0)
    mode_terms = rising[None] * (inner_sums + pole_decay * keep_mask[:, :, None, None] * prior_state[:, None])
    return mode_terms.reshape(-1, mode_terms.shape[2], mode_terms.shape[3])

def reference(projected, short_taps, pole_decay, residues, doc_lengths, cotangent):
    seq_len = projected.shape[1]
    chan_total = projected.shape[2]
    group_width = min(256, chan_total)
    group_count = chan_total // group_width
    tap_span = short_taps.shape[1] - 1
    doc_ids = doc_of(jnp.arange(seq_len, dtype=jnp.int32), doc_lengths)
    lead_docs = doc_of(jnp.arange(seq_len + tap_span, dtype=jnp.int32) - tap_span, doc_lengths)
    tail_docs = doc_of(jnp.arange(seq_len + tap_span, dtype=jnp.int32), doc_lengths)
    grad_scale = 1.0 / math.sqrt(seq_len)
    block_rows = min(64, seq_len)
    no_doc = jnp.int32(-1)

    def by_group(array):
        shaped = array.reshape(array.shape[:-1] + (group_count, group_width))
        return jnp.moveaxis(shaped, -2, 0)

    def one_group(inputs):
        proj_group, tap_group, decay_group, residue_group, cot_group = inputs
        zero_rows = jnp.zeros((3, tap_span, group_width), proj_group.dtype)
        extended = jnp.concatenate([zero_rows, proj_group], axis=1)
        features = featurize(extended, tap_group, lead_docs)
        carried = (features[1] * features[2]).astype(jnp.bfloat16)
        shrink = jnp.sqrt(1.0 - decay_group * decay_group)
        mode_coef = residue_group * shrink
        carry_zero = jnp.zeros(decay_group.shape, jnp.float32)
        mode_terms = finish(stretch_summary(carried, decay_group, doc_ids, no_doc, block_rows), decay_group, carry_zero)
        long_out = lax.optimization_barrier(jnp.sum(mode_terms * mode_coef[None], axis=1)).astype(jnp.bfloat16)
        gated_out = (features[0] * long_out.astype(jnp.float32)).astype(jnp.bfloat16)
        cot_float = cot_group.astype(jnp.float32)
        grad_q = cot_float * long_out.astype(jnp.float32)
        grad_long = (cot_float * features[0]).astype(jnp.bfloat16)
        back_terms = finish(stretch_summary(grad_long[::-1], decay_group, doc_ids[::-1], no_doc, block_rows), decay_group, carry_zero)
        grad_carried = lax.optimization_barrier(jnp.sum(back_terms * mode_coef[None], axis=1))[::-1].astype(jnp.bfloat16)
        grad_res = shrink * jnp.einsum('nmc,nc->mc', back_terms, carried[::-1].astype(jnp.float32), precision=lax.Precision.HIGHEST) * grad_scale
        carried_float = grad_carried.astype(jnp.float32)
        grad_feats = jnp.stack([grad_q, carried_float * features[2], carried_float * features[1]])
        zero_tail = jnp.zeros((3, tap_span, group_width), jnp.float32)
        grad_proj = unfeaturize(jnp.concatenate([grad_feats, zero_tail], axis=1), tap_group, tail_docs).astype(jnp.bfloat16)
        grad_tap = tap_grads(grad_feats, extended, lead_docs) * grad_scale
        return (gated_out, grad_proj, grad_tap, grad_res)
    results = lax.map(one_group, (by_group(projected), by_group(short_taps), by_group(pole_decay), by_group(residues), by_group(cotangent)))

    def joined(array):
        moved = jnp.moveaxis(array, 0, -2)
        return moved.reshape(moved.shape[:-2] + (chan_total,))
    return (joined(results[0]), joined(results[1]), joined(results[2]), joined(results[3]))
```

```python
import functools
import math

import jax
import jax.numpy as jnp
from jax import lax
from jax.experimental import pallas as pl
from jax.experimental.pallas import tpu as pltpu
from jax.sharding import PartitionSpec as P

F32 = jnp.float32
BF16 = jnp.bfloat16
SUB = 8
LANES = 128
HALO = 16


def shift(block, distance, cyclic=False):
    count = lax.axis_size("ctx")
    route = [(i, i + distance) for i in range(count) if 0 <= i + distance < count]
    return lax.ppermute(block, "ctx", route)


def row(ref, *index):
    *lead, at = index
    return jnp.broadcast_to(ref[(*lead, pl.ds(at, 1), slice(None))], (SUB, LANES))


def doc_ends(lens_ref, docs):
    ends, total = [], jnp.int32(0)
    for d in range(docs):
        total = total + lens_ref[d]
        ends.append(total)
    return ends


def fill_keep(keep_ref, ends, start, steps, span):
    spread = lax.broadcasted_iota(jnp.int32, (SUB, LANES), 0) * steps + start
    for r in range(-span, steps + span + 1):
        token = spread + r
        starts = token == 0
        for end in ends:
            starts = jnp.logical_or(starts, token == end)
        keep_ref[r + span] = jnp.where(starts, 0.0, 1.0)


def fill_same(same_ref, keep_ref, steps, span):
    for r in range(steps + span):
        running = keep_ref[r + span]
        same_ref[0, r] = running
        for j in range(2, span + 1):
            running = running * keep_ref[r + span - j + 1]
            same_ref[j - 1, r] = running


def fill_order(order_ref, rows, steps, span):
    shape = order_ref.shape
    at = lax.broadcasted_iota(jnp.int32, shape, 0)
    col = lax.broadcasted_iota(jnp.int32, shape, 1)
    token = (at & (SUB - 1)) * steps + (at >> 3) - span
    held = jnp.where(col < rows, col, jnp.where(col < rows + HALO, col - rows - HALO, col - HALO))
    order_ref[...] = jnp.where(token == held, 1.0, 0.0).astype(BF16)


def fill_chunks(chunk_ref, order_ref, ext_ref, proj_ref, cot_ref, left_ref, right_ref):
    rows = proj_ref.shape[1]
    for i in range(4):
        at = pl.ds(i * LANES, LANES)
        ext_ref[pl.ds(0, rows), at] = proj_ref[i] if i < 3 else cot_ref[...]
        if i < 3:
            ext_ref[pl.ds(rows, HALO), at] = left_ref[i]
        ext_ref[pl.ds(rows + HALO, HALO), at] = right_ref[i]
    chunk_ref[...] = jnp.dot(order_ref[...], ext_ref[...], preferred_element_type=F32)


def states_kernel(
    steps, span, modes, docs, lens_ref, proj_ref, cot_ref, left_ref, right_ref, taps_ref, pole_ref,
    feat_ref, chunk_state_ref, edge_ref,
    keep_ref, same_ref, order_ref, ext_ref, chunk_ref,
):
    rows = proj_ref.shape[1]
    start = lax.axis_index("ctx") * rows

    @pl.when(pl.program_id(0) == 0)
    def _():
        fill_keep(keep_ref, doc_ends(lens_ref, docs), start, steps, span)
        fill_same(same_ref, keep_ref, steps, span)
        fill_order(order_ref, rows, steps, span)
        ext_ref[...] = jnp.zeros_like(ext_ref)

    fill_chunks(chunk_ref, order_ref, ext_ref, proj_ref, cot_ref, left_ref, right_ref)

    def chunk(i, r):
        return chunk_ref[pl.ds((r + span) * SUB, SUB), pl.ds(i * LANES, LANES)]

    for i in range(3):
        taps = [row(taps_ref, i, j) for j in range(span + 1)]
        for r in range(steps + span):
            value = taps[0] * chunk(i, r)
            for j in range(1, span + 1):
                value = value + taps[j] * (same_ref[j - 1, r] * chunk(i, r - j))
            feat_ref[i, pl.ds(r * SUB, SUB), :] = value

    def feat(i, r):
        return feat_ref[i, pl.ds(r * SUB, SUB), :]

    poles = [row(pole_ref, m) for m in range(modes)]
    for way in range(2):
        state = [jnp.zeros((SUB, LANES), F32)] * modes
        through = jnp.ones((SUB, LANES), F32)
        order = range(steps) if way == 0 else range(steps + span - 1, span - 1, -1)
        for r in order:
            if way == 0:
                keep, source = keep_ref[r + span], feat(1, r) * feat(2, r)
            else:
                keep, source = keep_ref[r + 1 + span], feat(0, r) * chunk(3, r)
            through = through * keep
            state = [(poles[m] * keep) * state[m] + source for m in range(modes)]
        for m in range(modes):
            chunk_state_ref[way, m] = state[m]
            full, open_ = poles[m], through
            for _ in range(int(math.log2(steps))):
                full = full * full
            total = state[m]
            for hop in (1, 2, 4):
                move = hop if way == 0 else SUB - hop
                total = total + (full * open_) * pltpu.roll(total, move, 0)
                open_ = open_ * pltpu.roll(open_, move, 0)
                full = full * full
            edge = SUB - 1 if way == 0 else 0
            edge_ref[way, pl.ds(m, 1), :] = total[edge : edge + 1]


def finish_kernel(
    steps, span, modes, docs, lens_ref, proj_ref, cot_ref, left_ref, right_ref, taps_ref, pole_ref, res_ref,
    feat_ref, chunk_state_ref, states_ref,
    gated_ref, grad_proj_ref, sums_ref,
    keep_ref, same_ref, order_ref, ext_ref, chunk_ref, back_ref, incoming_ref, coef_ref, grad_ref, out_ref,
):
    rows = proj_ref.shape[1]
    me = lax.axis_index("ctx")
    shards = states_ref.shape[0]
    start = me * rows
    tile = pl.program_id(0)
    tiles = states_ref.shape[2] // LANES

    @pl.when(tile == 0)
    def _():
        ends = doc_ends(lens_ref, docs)
        fill_keep(keep_ref, ends, start, steps, span)
        fill_same(same_ref, keep_ref, steps, span)
        fill_order(order_ref, rows, steps, span)
        ext_ref[...] = jnp.zeros_like(ext_ref)
        at = lax.broadcasted_iota(jnp.int32, back_ref.shape, 0)
        col = lax.broadcasted_iota(jnp.int32, back_ref.shape, 1)
        back_ref[...] = jnp.where(at == (col & (SUB - 1)) * steps + (col >> 3), 1.0, 0.0).astype(BF16)

        last_start, next_start = jnp.int32(0), jnp.int32(shards * rows)
        resume = start + rows + span
        for end in ends:
            last_start = jnp.where(end <= start - 1, jnp.maximum(last_start, end), last_start)
            next_start = jnp.where(end > resume, jnp.minimum(next_start, end), next_start)
        first = last_start // rows
        last = jnp.minimum(shards - 1, lax.div(next_start - span - 1, rows))
        full = pole_ref[...]
        for _ in range(int(math.log2(rows))):
            full = full * full
        zero = jnp.zeros(full.shape, F32)
        incoming = lax.fori_loop(first, me, lambda j, s: full * s + states_ref[j], zero)
        back = lax.fori_loop(me + 1, last + 1, lambda j, s: full * s + states_ref[last + me + 1 - j], zero)
        for n in range(tiles):
            incoming_ref[n, 0] = incoming[:, n * LANES : (n + 1) * LANES]
            incoming_ref[n, 1] = back[:, n * LANES : (n + 1) * LANES]

    fill_chunks(chunk_ref, order_ref, ext_ref, proj_ref, cot_ref, left_ref, right_ref)

    def chunk(i, r):
        return chunk_ref[pl.ds((r + span) * SUB, SUB), pl.ds(i * LANES, LANES)]

    def feat(i, r):
        return feat_ref[i, pl.ds(r * SUB, SUB), :]

    lane_at = pl.ds(pl.multiple_of(tile * LANES, LANES), LANES)
    pole_rows = pole_ref[:, lane_at]
    shrink = jnp.sqrt(1.0 - pole_rows * pole_rows)
    coef_ref[0] = pole_rows
    coef_ref[1] = res_ref[...] * shrink
    coef_ref[2] = shrink
    poles = [row(coef_ref, 0, m) for m in range(modes)]
    sub = lax.broadcasted_iota(jnp.int32, (SUB, LANES), 0)
    scale = 1.0 / math.sqrt(shards * rows)
    taps_count = span + 1

    sums_ref[...] = jnp.zeros_like(sums_ref)

    for way in range(2):
        through = jnp.ones((SUB, LANES), F32)
        for r in range(steps):
            through = through * keep_ref[r + span if way == 0 else r + 2 * span + 1]
        head = 0 if way == 0 else SUB - 1
        state = []
        for m in range(modes):
            full = poles[m]
            for _ in range(int(math.log2(steps))):
                full = full * full
            entry = row(incoming_ref, tile, way, m)
            open_ = through
            total = chunk_state_ref[way, m]
            total = jnp.where(sub == head, total + (full * open_) * entry, total)
            for hop in (1, 2, 4):
                move = hop if way == 0 else SUB - hop
                inside = sub >= hop if way == 0 else sub < SUB - hop
                total = total + jnp.where(inside, (full * open_) * pltpu.roll(total, move, 0), 0.0)
                open_ = open_ * jnp.where(inside, pltpu.roll(open_, move, 0), 1.0)
                full = full * full
            state.append(jnp.where(sub == head, entry, pltpu.roll(total, 1 if way == 0 else SUB - 1, 0)))
        coefs = [row(coef_ref, 1, m) for m in range(modes)]
        if way == 0:
            for r in range(steps + span):
                keep = keep_ref[r + span]
                source = feat(1, r) * feat(2, r)
                state = [(poles[m] * keep) * state[m] + source for m in range(modes)]
                value = coefs[0] * state[0]
                for m in range(1, modes):
                    value = value + coefs[m] * state[m]
                grad_ref[0, r] = chunk(3, r) * value
                if r < steps:
                    out_ref[pl.ds(r * SUB, SUB), pl.ds(3 * LANES, LANES)] = feat(0, r) * value
        else:
            res_sums = [jnp.zeros((SUB, LANES), F32)] * modes
            for r in range(steps + span - 1, -1, -1):
                keep = keep_ref[r + 1 + span]
                source = chunk(3, r) * feat(0, r)
                state = [(poles[m] * keep) * state[m] + source for m in range(modes)]
                value = coefs[0] * state[0]
                for m in range(1, modes):
                    value = value + coefs[m] * state[m]
                grad_ref[1, r] = value * feat(2, r)
                grad_ref[2, r] = value * feat(1, r)
                if r < steps:
                    carried = feat(1, r) * feat(2, r)
                    res_sums = [res_sums[m] + carried * state[m] for m in range(modes)]
            for m in range(modes):
                total = jnp.sum(res_sums[m], axis=0, keepdims=True)
                sums_ref[pl.ds(3 * taps_count + m, 1), :] = total * coef_ref[2, pl.ds(m, 1), :] * scale

    for i in range(3):
        taps = [row(taps_ref, i, j) for j in range(taps_count)]
        tap_sums = [jnp.zeros((SUB, LANES), F32)] * taps_count
        grads = [jnp.zeros((SUB, LANES), F32)] * taps_count
        for r in range(steps + span):
            here = grad_ref[i, r]
            for j in range(taps_count):
                if r - j >= steps:
                    continue
                masked = here if j == 0 else same_ref[j - 1, r] * here
                if r < steps:
                    tap_sums[j] = tap_sums[j] + masked * chunk(i, r - j)
                if r - j >= 0:
                    grads[j] = grads[j] + taps[j] * masked
            done = r - span
            if done >= 0:
                out_ref[pl.ds(done * SUB, SUB), pl.ds(i * LANES, LANES)] = grads[span]
            grads = [jnp.zeros((SUB, LANES), F32)] + grads[:span]
        for j in range(taps_count):
            total = jnp.sum(tap_sums[j], axis=0, keepdims=True)
            sums_ref[pl.ds(i * taps_count + j, 1), :] = total * scale

    natural = jnp.dot(back_ref[...], out_ref[...].astype(BF16), preferred_element_type=F32).astype(BF16)
    gated_ref[...] = natural[:, 3 * LANES :]
    for i in range(3):
        grad_proj_ref[i] = natural[:, i * LANES : (i + 1) * LANES]


def per_device(projected, short_taps, pole_decay, residues, doc_lengths, cotangent):
    rows, chans = projected.shape[1:]
    span = short_taps.shape[1] - 1
    modes = pole_decay.shape[0]
    docs = doc_lengths.shape[0]
    shards = lax.axis_size("ctx")
    me = lax.axis_index("ctx")
    steps = rows // SUB
    tiles = chans // LANES
    ext_rows = -(-(rows + 2 * HALO) // LANES) * LANES
    sum_rows = 32

    left = shift(projected[:, rows - HALO :], 1)
    right = shift(jnp.concatenate([projected[:, :HALO], cotangent[None, :HALO]]), -1)

    smem = pl.BlockSpec(memory_space=pltpu.SMEM)

    def lanes(*lead):
        return pl.BlockSpec((*lead, LANES), lambda n: (*(0 for _ in lead), n))

    def whole(*shape):
        return pl.BlockSpec(shape, lambda n: tuple(0 for _ in shape))

    shared = [
        smem, lanes(3, rows), lanes(rows), lanes(3, HALO), lanes(4, HALO), lanes(3, span + 1),
    ]
    scratch = [
        pltpu.VMEM((steps + 2 * span + 1, SUB, LANES), F32),
        pltpu.VMEM((span, steps + span, SUB, LANES), F32),
        pltpu.VMEM(((steps + 2 * span) * SUB, ext_rows), BF16),
        pltpu.VMEM((ext_rows, 4 * LANES), BF16),
        pltpu.VMEM(((steps + 2 * span) * SUB, 4 * LANES), F32),
    ]
    params = pltpu.CompilerParams(vmem_limit_bytes=40 << 20)
    feat_spec = lanes(3, (steps + span) * SUB)
    chunk_state_spec = lanes(2, modes, SUB)

    feats, chunk_states, edges = pl.pallas_call(
        functools.partial(states_kernel, steps, span, modes, docs),
        grid=(tiles,),
        out_shape=(
            jax.ShapeDtypeStruct((3, (steps + span) * SUB, chans), F32),
            jax.ShapeDtypeStruct((2, modes, SUB, chans), F32),
            jax.ShapeDtypeStruct((2, modes, chans), F32),
        ),
        in_specs=shared + [lanes(modes)],
        out_specs=(feat_spec, chunk_state_spec, lanes(2, modes)),
        scratch_shapes=scratch,
        compiler_params=params,
        name="states",
    )(doc_lengths, projected, cotangent, left, right, short_taps, pole_decay)

    later = (jnp.arange(shards, dtype=jnp.int32) > me)[:, None, None]
    outgoing = jnp.where(later, edges[:1], edges[1:]).astype(BF16)
    states = lax.all_to_all(outgoing, "ctx", split_axis=0, concat_axis=0, tiled=True).astype(F32)

    gated, grad_proj, sums = pl.pallas_call(
        functools.partial(finish_kernel, steps, span, modes, docs),
        grid=(tiles,),
        out_shape=(
            jax.ShapeDtypeStruct((rows, chans), BF16),
            jax.ShapeDtypeStruct((3, rows, chans), BF16),
            jax.ShapeDtypeStruct((sum_rows, chans), F32),
        ),
        in_specs=shared
        + [whole(modes, chans), lanes(modes), feat_spec, chunk_state_spec, whole(shards, modes, chans)],
        out_specs=(lanes(rows), lanes(3, rows), lanes(sum_rows)),
        scratch_shapes=scratch
        + [
            pltpu.VMEM((rows, rows), BF16),
            pltpu.VMEM((tiles, 2, modes, LANES), F32),
            pltpu.VMEM((3, modes, LANES), F32),
            pltpu.VMEM((3, steps + span, SUB, LANES), F32),
            pltpu.VMEM((rows, 4 * LANES), F32),
        ],
        compiler_params=params,
        name="finish",
    )(doc_lengths, projected, cotangent, left, right, short_taps, pole_decay, residues, feats, chunk_states, states)

    near = 4
    far = shards // near

    def around(block, hop):
        return lax.ppermute(
            block, "ctx", [(i, i // near * near + (i + hop) % near) for i in range(shards)]
        )

    part = sums.astype(BF16)
    one, two, three = (around(part, hop).astype(F32) for hop in (1, 2, 3))
    part = ((part.astype(F32) + two) + (one + three)).astype(BF16)
    groups = [[f * near + n for f in range(far)] for n in range(near)]
    spread = lax.optimization_barrier(jnp.broadcast_to(part[None], (far, sum_rows, chans)))
    gathered = lax.all_to_all(spread, "ctx", 0, 0, tiled=True, axis_index_groups=groups)
    total = jnp.sum(gathered.astype(F32), axis=0)
    tap_rows = 3 * (span + 1)
    grad_tap = total[:tap_rows].reshape(3, span + 1, chans)
    grad_res = total[tap_rows : tap_rows + modes]
    return (gated, grad_proj, grad_tap, grad_res)


def solution(mesh):
    placed = (
        P(None, "ctx", "tp"),
        P(None, None, "tp"),
        P(None, "tp"),
        P(None, "tp"),
        P(),
        P("ctx", "tp"),
    )
    return jax.shard_map(
        per_device,
        mesh=mesh,
        in_specs=placed,
        out_specs=(P("ctx", "tp"), P(None, "ctx", "tp"), P(None, None, "tp"), P(None, "tp")),
        check_vma=False,
    )
```

```python
import functools
import math

import jax
import jax.numpy as jnp
from jax import lax
from jax.experimental import pallas as pl
from jax.experimental.pallas import tpu as pltpu
from jax.sharding import PartitionSpec as P

F32 = jnp.float32
BF16 = jnp.bfloat16
SUB = 8
LANES = 128
HALO = 16
SUM_ROWS = 32


def shift(block, distance):
    count = lax.axis_size("ctx")
    route = [(i, i + distance) for i in range(count) if 0 <= i + distance < count]
    return lax.ppermute(block, "ctx", route)


def spread(line):
    return jnp.broadcast_to(line, (SUB, LANES))


def power(base, exponent):
    for _ in range(int(math.log2(exponent))):
        base = base * base
    return base


def total_of(terms):
    terms = list(terms)
    while len(terms) > 1:
        terms = [a + b for a, b in zip(terms[::2], terms[1::2])] + terms[len(terms) & ~1 :]
    return terms[0]


def doc_ends(lens_ref):
    ends, total = [], jnp.int32(0)
    for d in range(lens_ref.shape[0]):
        total = total + lens_ref[d]
        ends.append(total)
    return ends


def keep_at(token, ends):
    starts = token == 0
    for end in ends:
        starts = jnp.logical_or(starts, token == end)
    return jnp.where(starts, 0.0, 1.0)


def fill_keep(keep_ref, ends, start, steps, span):
    token = lax.broadcasted_iota(jnp.int32, (SUB, LANES), 0) * steps + start
    for r in range(-span, steps + span + 1):
        keep_ref[r + span] = keep_at(token + r, ends)


def fill_same(same_ref, keep_ref, steps, span):
    for r in range(steps + span):
        running = keep_ref[r + span]
        same_ref[0, r] = running
        for j in range(2, span + 1):
            running = running * keep_ref[r + span - j + 1]
            same_ref[j - 1, r] = running


def fill_cum(cum_ref, keep_ref, steps, span):
    running = jnp.ones((SUB, LANES), F32)
    for r in range(steps + span):
        running = running * keep_ref[r + span]
        cum_ref[0, r] = running
    running = jnp.ones((SUB, LANES), F32)
    for r in range(steps + span - 1, -1, -1):
        running = running * keep_ref[r + 1 + span]
        cum_ref[1, r] = running


def fill_pick(pick_ref, ends, start, rows, span):
    shards = pick_ref.shape[1]
    last_start, next_start = jnp.int32(0), jnp.int32(shards * rows)
    for end in ends:
        last_start = jnp.where(end < start, jnp.maximum(last_start, end), last_start)
        next_start = jnp.where(end > start + rows + span, jnp.minimum(next_start, end), next_start)
    owner = lax.broadcasted_iota(jnp.int32, (shards, LANES), 0) * rows
    pick_ref[0] = jnp.where(owner + rows > last_start, 1.0, 0.0)
    pick_ref[1] = jnp.where(owner + span < next_start, 1.0, 0.0)


def fill_order(order_ref, rows, steps, span):
    shape = order_ref.shape
    at = lax.broadcasted_iota(jnp.int32, shape, 0)
    col = lax.broadcasted_iota(jnp.int32, shape, 1)
    token = (at & (SUB - 1)) * steps + (at >> 3) - span
    held = jnp.where(col < rows, col, jnp.where(col < rows + HALO, col - rows - HALO, col - HALO))
    order_ref[...] = jnp.where(token == held, 1.0, 0.0).astype(BF16)


def fill_rim_masks(mask_ref, ends, start, rows, span):
    last_start, next_start = jnp.int32(0), jnp.int32(1 << 30)
    for end in ends:
        last_start = jnp.where(end < start + rows, jnp.maximum(last_start, end), last_start)
        next_start = jnp.where(end > start + span, jnp.minimum(next_start, end), next_start)
    sub = lax.broadcasted_iota(jnp.int32, (SUB, LANES), 0)
    for side in range(2):
        token = start + sub + side * rows
        running = jnp.ones((SUB, LANES), F32)
        for j in range(span):
            running = running * keep_at(token - j, ends)
            mask_ref[side, j] = running
        seen = token >= last_start if side == 0 else token < next_start
        mask_ref[side, span] = jnp.where(jnp.logical_and(sub < span, seen), 1.0, 0.0)


def at_step(r):
    return pl.ds(r * SUB, SUB)


def lanes_of(i):
    return pl.ds(i * LANES, LANES)


def load_kernel(
    steps, span,
    lens_hbm, proj_hbm, cot_hbm, taps_hbm, pole_hbm, res_hbm,
    left_ref, right_ref, proj_ref, cot_ref, taps_ref, pole_ref, res_ref, keep_ref, rim_mask_ref, pick_ref, order_ref,
    lens_ref, edge_sem, small_sem, tile_sem,
):
    tiles, _, rows, _ = proj_ref.shape
    lens_copy = pltpu.make_async_copy(lens_hbm, lens_ref, small_sem.at[0])
    copies = [
        pltpu.make_async_copy(proj_hbm.at[:, pl.ds(rows - HALO, HALO), :], left_ref, edge_sem.at[0]),
        pltpu.make_async_copy(proj_hbm.at[:, pl.ds(0, HALO), :], right_ref.at[pl.ds(0, 3)], edge_sem.at[1]),
        pltpu.make_async_copy(cot_hbm.at[pl.ds(0, HALO), :], right_ref.at[3], edge_sem.at[2]),
        pltpu.make_async_copy(taps_hbm, taps_ref, small_sem.at[1]),
        pltpu.make_async_copy(pole_hbm, pole_ref, small_sem.at[2]),
        pltpu.make_async_copy(res_hbm, res_ref, small_sem.at[3]),
    ]
    for n in range(tiles):
        at = lanes_of(n)
        copies.append(pltpu.make_async_copy(proj_hbm.at[:, :, at], proj_ref.at[n], tile_sem.at[n, 0]))
        copies.append(pltpu.make_async_copy(cot_hbm.at[:, at], cot_ref.at[n], tile_sem.at[n, 1]))
    lens_copy.start()
    for copy in copies:
        copy.start()
    fill_order(order_ref, rows, steps, span)
    lens_copy.wait()
    start = lax.axis_index("ctx") * rows
    ends = doc_ends(lens_ref)
    fill_keep(keep_ref, ends, start, steps, span)
    fill_rim_masks(rim_mask_ref, ends, start, rows, span)
    fill_pick(pick_ref, ends, start, rows, span)
    for copy in copies:
        copy.wait()


def fill_ext(ext_ref, n, proj_ref, cot_ref, left_ref, right_ref, streams):
    rows = proj_ref.shape[2]
    lane_at = pl.ds(pl.multiple_of(n * LANES, LANES), LANES)
    for place, i in enumerate(streams):
        at = lanes_of(place)
        ext_ref[pl.ds(0, rows), at] = proj_ref[n, i] if i < 3 else cot_ref[n]
        if i < 3:
            ext_ref[pl.ds(rows, HALO), at] = left_ref[i, :, lane_at]
        ext_ref[pl.ds(rows + HALO, HALO), at] = right_ref[i, :, lane_at]


def edges_kernel(
    steps, span, modes,
    proj_ref, cot_ref, taps_ref, pole_ref, keep_ref, order_ref,
    edge_ref, rim_ref,
    same_ref, mask_ref, ext_ref, chunk_ref, feat_ref,
):
    tiles, _, rows, _ = proj_ref.shape
    fill_same(same_ref, keep_ref, steps, span)
    sub = lax.broadcasted_iota(jnp.int32, (SUB, LANES), 0)
    running = jnp.ones((SUB, LANES), F32)
    for r in range(steps - 1, -1, -1):
        mask_ref[0, r] = running if r >= span else jnp.where(sub == 0, 0.0, running)
        running = running * keep_ref[r + span]
    through = [running]
    running = jnp.ones((SUB, LANES), F32)
    for r in range(span, steps + span):
        mask_ref[1, r - span] = running if r < steps else jnp.where(sub == SUB - 1, 0.0, running)
        running = running * keep_ref[r + 1 + span]
    through.append(running)

    def tile_step(n, carry):
        for i in range(4):
            ext_ref[:, lanes_of(i)] = proj_ref[n, i] if i < 3 else cot_ref[n]
        chunk_ref[...] = jnp.dot(order_ref[:, pl.ds(0, rows)], ext_ref[...], preferred_element_type=F32)
        rim_ref[n, 0] = proj_ref[n, 1, pl.ds(0, HALO), :].astype(F32)[:SUB]
        rim_ref[n, 1] = proj_ref[n, 2, pl.ds(0, HALO), :].astype(F32)[:SUB]
        rim_ref[n, 2] = proj_ref[n, 0, pl.ds(rows - HALO, HALO), :].astype(F32)[HALO - SUB :]

        def chunk(i, r):
            return chunk_ref[at_step(r + span), lanes_of(i)]

        lane_at = pl.ds(pl.multiple_of(n * LANES, LANES), LANES)
        for i in range(3):
            taps = [spread(taps_ref[i, pl.ds(j, 1), lane_at]) for j in range(span + 1)]
            first = span if i == 0 else 0
            for r in range(first, first + steps):
                value = taps[0] * chunk(i, r)
                for j in range(1, span + 1):
                    value = value + taps[j] * (same_ref[j - 1, r] * chunk(i, r - j))
                if i == 0:
                    value = value * chunk(3, r) * mask_ref[1, r - first]
                elif i == 2:
                    value = value * feat_ref[1, r] * mask_ref[0, r]
                feat_ref[i, r - first] = value

        poles = [spread(pole_ref[pl.ds(m, 1), lane_at]) for m in range(modes)]
        for way in range(2):
            state = [jnp.zeros((SUB, LANES), F32)] * modes
            for r in range(steps) if way == 0 else range(steps - 1, -1, -1):
                source = feat_ref[2 if way == 0 else 0, r]
                state = [poles[m] * state[m] + source for m in range(modes)]
            open_ = through[way]
            factors = [power(poles[m], steps) for m in range(modes)]
            for hop in (1, 2, 4):
                move = hop if way == 0 else SUB - hop
                for m in range(modes):
                    state[m] = state[m] + (factors[m] * open_) * pltpu.roll(state[m], move, 0)
                    factors[m] = factors[m] * factors[m]
                open_ = open_ * pltpu.roll(open_, move, 0)
            last = SUB - 1 if way == 0 else 0
            for m in range(modes):
                edge_ref[way, pl.ds(m, 1), lane_at] = state[m][last : last + 1]
        return carry

    lax.fori_loop(0, tiles, tile_step, 0)


def rims_kernel(
    rows, span, modes,
    edge_ref, rim_ref, taps_ref, pole_ref, mask_ref, left_ref, right_ref,
    send_ref,
    ext_ref, line_ref, out_ref,
):
    tiles = rim_ref.shape[0]
    for n in range(tiles):
        at = lanes_of(n)
        ext_ref[0, pl.ds(0, SUB)] = left_ref[1, :, at].astype(F32)[HALO - SUB :]
        ext_ref[0, pl.ds(SUB, SUB)] = rim_ref[n, 0]
        ext_ref[1, pl.ds(0, SUB)] = left_ref[2, :, at].astype(F32)[HALO - SUB :]
        ext_ref[1, pl.ds(SUB, SUB)] = rim_ref[n, 1]
        ext_ref[2, pl.ds(0, SUB)] = rim_ref[n, 2]
        ext_ref[2, pl.ds(SUB, SUB)] = right_ref[0, :, at].astype(F32)[:SUB]
        made = []
        for e, i, side in ((0, 1, 0), (1, 2, 0), (2, 0, 1)):
            value = spread(taps_ref[i, pl.ds(0, 1), at]) * ext_ref[e, pl.ds(SUB, SUB)]
            for j in range(1, span + 1):
                value = value + spread(taps_ref[i, pl.ds(j, 1), at]) * (
                    mask_ref[side, j - 1] * ext_ref[e, pl.ds(SUB - j, SUB)]
                )
            made.append(value)
        line_ref[n, 0] = made[0] * made[1] * mask_ref[0, span]
        line_ref[n, 1] = made[2] * right_ref[3, :, at].astype(F32)[:SUB] * mask_ref[1, span]
        pole = pole_ref[:, at]
        scale, bit, left_over = jnp.ones((modes, LANES), F32), pole, rows - span
        while left_over:
            if left_over & 1:
                scale = scale * bit
            bit = bit * bit
            left_over >>= 1
        for way in range(2):
            running = jnp.zeros((modes, LANES), F32)
            for t in range(span) if way == 0 else range(span - 1, -1, -1):
                running = running * pole + spread(line_ref[n, way, pl.ds(t, 1), :])
            out_ref[way, :, at] = edge_ref[way, :, at] + scale * running
    half = out_ref.shape[2] // 2
    ahead, behind = (
        jnp.concatenate([out_ref[way, :, pl.ds(0, half)], out_ref[way, :, pl.ds(half, half)]], axis=0).astype(BF16)
        for way in range(2)
    )
    me = lax.axis_index("ctx")

    def fill(value):
        def one(d, carry):
            send_ref[d] = value
            return carry

        return one

    lax.fori_loop(0, me, fill(behind), 0)
    lax.fori_loop(me, send_ref.shape[0], fill(ahead), 0)


def local_kernel(
    steps, span, modes,
    proj_ref, cot_ref, left_ref, right_ref, taps_ref, pole_ref, res_ref, keep_ref, order_ref,
    feat_ref, sums_ref, pack_hbm, query_hbm,
    same_ref, ext_ref, chunk_ref, coef_ref, pack_ref, query_ref, out_sem,
):
    tiles, _, rows, _ = proj_ref.shape
    full_steps = steps + span
    fill_same(same_ref, keep_ref, steps, span)
    ext_ref[...] = jnp.zeros_like(ext_ref)
    sub = lax.broadcasted_iota(jnp.int32, (SUB, LANES), 0)

    def run(first, count):
        running = keep_ref[first + span]
        for r in range(first + 1, first + count):
            running = running * keep_ref[r + span]
        return running

    through = [run(0, steps), run(span + 1, steps)]
    onward = run(steps, span + 1)

    def tile_results(n):
        return (
            pltpu.make_async_copy(pack_ref.at[n], pack_hbm.at[n], out_sem.at[n, 0]),
            pltpu.make_async_copy(query_ref.at[n], query_hbm.at[n], out_sem.at[n, 1]),
        )

    def tile_step(n, carry):
        lane_at = pl.ds(pl.multiple_of(n * LANES, LANES), LANES)
        fill_ext(ext_ref, n, proj_ref, cot_ref, left_ref, right_ref, range(4))
        chunk_ref[...] = jnp.dot(order_ref[...], ext_ref[...], preferred_element_type=F32)

        def chunk(i, r):
            return chunk_ref[at_step(r + span), lanes_of(i)]

        for i in range(3):
            taps = [spread(taps_ref[i, pl.ds(j, 1), lane_at]) for j in range(span + 1)]
            for r in range(full_steps):
                value = taps[0] * chunk(i, r)
                for j in range(1, span + 1):
                    value = value + taps[j] * (same_ref[j - 1, r] * chunk(i, r - j))
                if i == 0:
                    query_ref[n, r] = value
                else:
                    feat_ref[n, i - 1, r] = value

        pole_rows = pole_ref[:, lane_at]
        coef_ref[...] = res_ref[:, lane_at] * jnp.sqrt(1.0 - pole_rows * pole_rows)
        poles = [spread(pole_ref[pl.ds(m, 1), lane_at]) for m in range(modes)]
        coefs = [spread(coef_ref[pl.ds(m, 1), :]) for m in range(modes)]
        ends = []
        res_sums = [jnp.zeros((SUB, LANES), F32)] * modes
        for way in range(2):
            state = [jnp.zeros((SUB, LANES), F32)] * modes
            for r in range(full_steps) if way == 0 else range(full_steps - 1, -1, -1):
                if way == 0:
                    keep, source = keep_ref[r + span], feat_ref[n, 0, r] * feat_ref[n, 1, r]
                else:
                    keep, source = keep_ref[r + 1 + span], chunk(3, r) * query_ref[n, r]
                state = [(poles[m] * keep) * state[m] + source for m in range(modes)]
                pack_ref[n, way * full_steps + r] = total_of(coefs[m] * state[m] for m in range(modes))
                if way == 0 and r == steps - 1 or way == 1 and r == span:
                    ends.append(state)
                if way == 1 and r < steps:
                    carried = feat_ref[n, 0, r] * feat_ref[n, 1, r]
                    res_sums = [res_sums[m] + carried * state[m] for m in range(modes)]

        for way in range(2):
            head = 0 if way == 0 else SUB - 1
            back = 1 if way == 0 else SUB - 1
            for m in range(modes):
                state = ends[way][m]
                factor = power(poles[m], steps)
                open_ = through[way]
                unit = factor * open_
                for hop in (1, 2, 4):
                    move = hop if way == 0 else SUB - hop
                    inside = sub >= hop if way == 0 else sub < SUB - hop
                    far = jnp.where(inside, pltpu.roll(state, move, 0), 0.0)
                    state = state + (factor * open_) * far
                    unit = unit * jnp.where(inside, pltpu.roll(unit, move, 0), 1.0)
                    open_ = open_ * jnp.where(inside, pltpu.roll(open_, move, 0), 1.0)
                    factor = factor * factor
                state = jnp.where(sub == head, 0.0, pltpu.roll(state, back, 0))
                unit = jnp.where(sub == head, 1.0, pltpu.roll(unit, back, 0))
                at = 2 * full_steps + way * 2 * modes + m
                pack_ref[n, at] = coefs[m] * state
                pack_ref[n, at + modes] = coefs[m] * unit
                if way == 1:
                    reach = poles[m]
                    for _ in range(span):
                        reach = reach * poles[m]
                    seen = reach * onward * ends[0][m]
                    total = jnp.sum(res_sums[m] + seen * state, axis=0, keepdims=True)
                    sums_ref[0, pl.ds(m, 1), lane_at] = total
                    sums_ref[1, pl.ds(m, 1), lane_at] = jnp.sum(seen * unit, axis=0, keepdims=True)
        for copy in tile_results(n):
            copy.start()
        return carry

    lax.fori_loop(0, tiles, tile_step, 0)
    for n in range(tiles):
        for copy in tile_results(n):
            copy.wait()


def fill_coming(coming_ref, states_ref, pick_ref, pole_ref, rows):
    shards = states_ref.shape[0]
    me = lax.axis_index("ctx")
    modes, chans = pole_ref.shape
    full = power(pole_ref[...], rows)
    half = chans // 2
    full = jnp.concatenate([full[:, :half], full[:, half:]], axis=0)

    def seen(way, j):
        return jnp.broadcast_to(pick_ref[way, pl.ds(j, 1), pl.ds(0, 1)], full.shape)

    def forward(j, state):
        return full * state + seen(0, j) * states_ref[j].astype(F32)

    def backward(n, state):
        j = shards - 1 - n
        return full * state + seen(1, j) * states_ref[j].astype(F32)

    zero = jnp.zeros(full.shape, F32)
    coming = lax.fori_loop(0, me, forward, zero)
    back = lax.fori_loop(0, shards - 1 - me, backward, zero)
    for way, state in enumerate((coming, back)):
        for n in range(chans // LANES):
            top, left = divmod(n * LANES, half)
            coming_ref[n, way] = state[top * modes : (top + 1) * modes, left : left + LANES]


def combine(way, n, steps, span, modes, pole_ref, pack_ref, coming_ref, cum_ref, lane_at):
    full_steps = steps + span
    poles = [spread(pole_ref[pl.ds(m, 1), lane_at]) for m in range(modes)]
    at = 2 * full_steps + way * 2 * modes
    state = [
        pack_ref[n, at + m] + pack_ref[n, at + modes + m] * spread(coming_ref[n, way, pl.ds(m, 1), :])
        for m in range(modes)
    ]
    for r in range(full_steps) if way == 0 else range(full_steps - 1, -1, -1):
        state = [poles[m] * state[m] for m in range(modes)]
        yield r, pack_ref[n, way * full_steps + r] + cum_ref[way, r] * total_of(state)


def sums_kernel(
    rows, steps, span, modes,
    proj_ref, cot_ref, left_ref, right_ref, pole_ref, keep_ref, order_ref, pick_ref, states_ref, feat_ref, res_ref,
    pack_hbm,
    out_ref,
    pack_ref, same_ref, cum_ref, ext_ref, chunk_ref, coming_ref, grad_ref, sums_ref, tile_sem,
):
    tiles = feat_ref.shape[0]
    shards = states_ref.shape[0]

    def load(n):
        return pltpu.make_async_copy(pack_hbm.at[n], pack_ref.at[n], tile_sem.at[n])

    for n in range(tiles):
        load(n).start()
    fill_same(same_ref, keep_ref, steps, span)
    fill_cum(cum_ref, keep_ref, steps, span)
    ext_ref[...] = jnp.zeros_like(ext_ref)
    sums_ref[...] = jnp.zeros_like(sums_ref)
    fill_coming(coming_ref, states_ref, pick_ref, pole_ref, rows)
    scale = 1.0 / math.sqrt(shards * rows)
    for n in range(tiles):
        at = lanes_of(n)
        pole = pole_ref[:, at]
        total = res_ref[0, :, at] + res_ref[1, :, at] * coming_ref[n, 1]
        sums_ref[pl.ds(3 * SUB, modes), at] = total * jnp.sqrt(1.0 - pole * pole) * scale

    def tile_step(n, carry):
        lane_at = pl.ds(pl.multiple_of(n * LANES, LANES), LANES)
        fill_ext(ext_ref, n, proj_ref, cot_ref, left_ref, right_ref, range(4))
        chunk_ref[...] = jnp.dot(order_ref[...], ext_ref[...], preferred_element_type=F32)
        load(n).wait()
        for way in range(2):
            for r, value in combine(way, n, steps, span, modes, pole_ref, pack_ref, coming_ref, cum_ref, lane_at):
                if r >= steps:
                    continue
                if way == 0:
                    grad_ref[0, r] = chunk_ref[at_step(r + span), lanes_of(3)] * value
                else:
                    grad_ref[1, r] = value * feat_ref[n, 1, r]
                    grad_ref[2, r] = value * feat_ref[n, 0, r]
        for i in range(3):
            tap_sums = [jnp.zeros((SUB, LANES), F32)] * (span + 1)
            for r in range(steps):
                here = grad_ref[i, r]
                for j in range(span + 1):
                    masked = here if j == 0 else same_ref[j - 1, r] * here
                    tap_sums[j] = tap_sums[j] + masked * chunk_ref[at_step(r - j + span), lanes_of(i)]
            for j in range(span + 1):
                sums_ref[pl.ds(i * SUB + j, 1), lane_at] = jnp.sum(tap_sums[j], axis=0, keepdims=True) * scale
        return carry

    lax.fori_loop(0, tiles, tile_step, 0)
    out_ref[...] = sums_ref[...].astype(BF16)


def outputs_kernel(
    rows, steps, span, modes,
    proj_ref, cot_ref, left_ref, right_ref, taps_ref, pole_ref, keep_ref, order_ref, pick_ref, states_ref, feat_ref,
    pack_hbm, query_hbm,
    gated_ref, grad_proj_ref,
    pack_ref, query_ref, same_ref, cum_ref, ext_ref, chunk_ref, coming_ref, grad_ref, back_ref, out_ref, tile_sem,
):
    tiles = feat_ref.shape[0]

    def loads(n):
        return (
            pltpu.make_async_copy(pack_hbm.at[n], pack_ref.at[n], tile_sem.at[n, 0]),
            pltpu.make_async_copy(query_hbm.at[n], query_ref.at[n], tile_sem.at[n, 1]),
        )

    for n in range(tiles):
        for copy in loads(n):
            copy.start()
    fill_same(same_ref, keep_ref, steps, span)
    fill_cum(cum_ref, keep_ref, steps, span)
    ext_ref[...] = jnp.zeros_like(ext_ref)
    at = lax.broadcasted_iota(jnp.int32, back_ref.shape, 0)
    col = lax.broadcasted_iota(jnp.int32, back_ref.shape, 1)
    back_ref[...] = jnp.where(at == (col & (SUB - 1)) * steps + (col >> 3), 1.0, 0.0).astype(BF16)
    fill_coming(coming_ref, states_ref, pick_ref, pole_ref, rows)

    def tile_step(n, carry):
        lane_at = pl.ds(pl.multiple_of(n * LANES, LANES), LANES)
        fill_ext(ext_ref, n, proj_ref, cot_ref, left_ref, right_ref, (3,))
        chunk_ref[...] = jnp.dot(order_ref[...], ext_ref[...], preferred_element_type=F32)
        for copy in loads(n):
            copy.wait()
        for way in range(2):
            for r, value in combine(way, n, steps, span, modes, pole_ref, pack_ref, coming_ref, cum_ref, lane_at):
                if way == 0:
                    grad_ref[0, r] = chunk_ref[at_step(r + span), :] * value
                    if r < steps:
                        out_ref[at_step(r), lanes_of(3)] = query_ref[n, r] * value
                else:
                    grad_ref[1, r] = value * feat_ref[n, 1, r]
                    grad_ref[2, r] = value * feat_ref[n, 0, r]
        for i in range(3):
            taps = [spread(taps_ref[i, pl.ds(j, 1), lane_at]) for j in range(span + 1)]
            for r in range(steps):
                value = taps[0] * grad_ref[i, r]
                for j in range(1, span + 1):
                    value = value + taps[j] * (same_ref[j - 1, r + j] * grad_ref[i, r + j])
                out_ref[at_step(r), lanes_of(i)] = value
        natural = jnp.dot(back_ref[...], out_ref[...].astype(BF16), preferred_element_type=F32).astype(BF16)
        gated_ref[:, lane_at] = natural[:, 3 * LANES :]
        for i in range(3):
            grad_proj_ref[i, :, lane_at] = natural[:, i * LANES : (i + 1) * LANES]
        return carry

    lax.fori_loop(0, tiles, tile_step, 0)


def final_kernel(parts_ref, tap_ref, res_ref):
    total = total_of(parts_ref[g].astype(F32) for g in range(parts_ref.shape[0]))
    for i in range(3):
        tap_ref[i] = total[i * SUB : i * SUB + tap_ref.shape[1]]
    res_ref[...] = total[3 * SUB :]


def per_device(projected, short_taps, pole_decay, residues, doc_lengths, cotangent):
    rows, chans = projected.shape[1:]
    taps = short_taps.shape[1]
    span = taps - 1
    modes = pole_decay.shape[0]
    docs = doc_lengths.shape[0]
    shards = lax.axis_size("ctx")
    steps = rows // SUB
    tiles = chans // LANES
    full_steps = steps + span
    chunk_rows = (full_steps + span) * SUB
    ext_rows = -(-(rows + 2 * HALO) // LANES) * LANES
    pack_shape = (tiles, 2 * full_steps + 4 * modes, SUB, LANES)
    query_shape = (tiles, full_steps, SUB, LANES)

    vmem = pl.BlockSpec(memory_space=pltpu.VMEM)
    hbm = pl.BlockSpec(memory_space=pltpu.HBM)
    free = jax.ShapeDtypeStruct
    dma = pltpu.SemaphoreType.DMA

    def in_hbm(*arrays):
        return [pltpu.with_memory_space_constraint(a, pltpu.HBM) for a in arrays]

    def in_vmem(*arrays):
        return [pltpu.with_memory_space_constraint(a, pltpu.VMEM) for a in arrays]

    def call(kernel, name, out_shape, in_specs, scratch, limit, flops):
        return pl.pallas_call(
            kernel,
            out_shape=tuple(space(shape, kind) for shape, kind, space in out_shape),
            in_specs=in_specs,
            out_specs=tuple(hbm if o[2] is pltpu.HBM else vmem for o in out_shape),
            scratch_shapes=scratch,
            compiler_params=pltpu.CompilerParams(vmem_limit_bytes=limit << 20),
            cost_estimate=pl.CostEstimate(flops=flops, bytes_accessed=4 << 20, transcendentals=0),
            name=name,
        )

    same_scratch = pltpu.VMEM((span, full_steps, SUB, LANES), F32)
    cum_scratch = pltpu.VMEM((2, full_steps, SUB, LANES), F32)
    coming_scratch = pltpu.VMEM((tiles, 2, modes, LANES), F32)

    left, right, proj, cot, taps_near, poles, weights, keeps, rim_masks, picks, order = call(
        functools.partial(load_kernel, steps, span),
        "load",
        [
            ((3, HALO, chans), BF16, free),
            ((4, HALO, chans), BF16, free),
            ((tiles, 3, rows, LANES), BF16, pltpu.VMEM),
            ((tiles, rows, LANES), BF16, pltpu.VMEM),
            ((3, taps, chans), F32, pltpu.VMEM),
            ((modes, chans), F32, pltpu.VMEM),
            ((modes, chans), F32, pltpu.VMEM),
            ((full_steps + span + 1, SUB, LANES), F32, pltpu.VMEM),
            ((2, taps, SUB, LANES), F32, pltpu.VMEM),
            ((2, shards, LANES), F32, pltpu.VMEM),
            ((chunk_rows, ext_rows), BF16, pltpu.VMEM),
        ],
        [hbm] * 6,
        [pltpu.SMEM((docs,), jnp.int32), dma((3,)), dma((4,)), dma((tiles, 2))],
        8,
        1_000_000,
    )(*in_hbm(doc_lengths, projected, cotangent, short_taps, pole_decay, residues))
    left = shift(left, 1)
    right = shift(right, -1)

    edges, rims = call(
        functools.partial(edges_kernel, steps, span, modes),
        "edges",
        [((2, modes, chans), F32, pltpu.VMEM), ((tiles, 3, SUB, LANES), F32, pltpu.VMEM)],
        [vmem] * 6,
        [
            same_scratch,
            pltpu.VMEM((2, steps, SUB, LANES), F32),
            pltpu.VMEM((rows, 4 * LANES), BF16),
            pltpu.VMEM((chunk_rows, 4 * LANES), F32),
            pltpu.VMEM((3, steps, SUB, LANES), F32),
        ],
        12,
        40_000_000,
    )(*in_vmem(proj, cot, taps_near, poles, keeps, order))

    (outgoing,) = call(
        functools.partial(rims_kernel, rows, span, modes),
        "rims",
        [((shards, 2 * modes, chans // 2), BF16, free)],
        [vmem] * 7,
        [
            pltpu.VMEM((3, 2 * SUB, LANES), F32),
            pltpu.VMEM((tiles, 2, SUB, LANES), F32),
            pltpu.VMEM((2, modes, chans), F32),
        ],
        8,
        1_000_000,
    )(*in_vmem(edges, rims, taps_near, poles, rim_masks), left, right)

    states = lax.all_to_all(outgoing, "ctx", split_axis=0, concat_axis=0, tiled=True)

    feats, res_sums, pack, query = call(
        functools.partial(local_kernel, steps, span, modes),
        "local",
        [
            ((tiles, 2, full_steps, SUB, LANES), F32, pltpu.VMEM),
            ((2, modes, chans), F32, pltpu.VMEM),
            (pack_shape, F32, pltpu.HBM),
            (query_shape, F32, pltpu.HBM),
        ],
        [vmem] * 9,
        [
            same_scratch,
            pltpu.VMEM((ext_rows, 4 * LANES), BF16),
            pltpu.VMEM((chunk_rows, 4 * LANES), F32),
            pltpu.VMEM((modes, LANES), F32),
            pltpu.VMEM(pack_shape, F32),
            pltpu.VMEM(query_shape, F32),
            dma((tiles, 2)),
        ],
        16,
        60_000_000,
    )(*in_vmem(proj, cot), left, right, *in_vmem(taps_near, poles, weights, keeps, order))

    (sums,) = call(
        functools.partial(sums_kernel, rows, steps, span, modes),
        "sums",
        [((SUM_ROWS, chans), BF16, free)],
        [vmem] * 11 + [hbm],
        [
            pltpu.VMEM(pack_shape, F32),
            same_scratch,
            cum_scratch,
            pltpu.VMEM((ext_rows, 4 * LANES), BF16),
            pltpu.VMEM((chunk_rows, 4 * LANES), F32),
            coming_scratch,
            pltpu.VMEM((3, steps, SUB, LANES), F32),
            pltpu.VMEM((SUM_ROWS, chans), F32),
            dma((tiles,)),
        ],
        12,
        30_000_000,
    )(
        *in_vmem(proj, cot),
        left,
        right,
        *in_vmem(poles, keeps, order, picks),
        states,
        *in_vmem(feats, res_sums),
        *in_hbm(pack),
    )

    near = 4
    far = shards // near

    def around(block, hop):
        return lax.ppermute(
            block, "ctx", [(i, i // near * near + (i + hop) % near) for i in range(shards)]
        )

    one, two, three = (around(sums, hop).astype(F32) for hop in (1, 2, 3))
    part = ((sums.astype(F32) + two) + (one + three)).astype(BF16)
    groups = [[f * near + n for f in range(far)] for n in range(near)]
    spread_part = lax.optimization_barrier(jnp.broadcast_to(part[None], (far, SUM_ROWS, chans)))
    gathered = lax.all_to_all(spread_part, "ctx", 0, 0, tiled=True, axis_index_groups=groups)
    grad_tap, grad_res = call(
        final_kernel,
        "final",
        [((3, taps, chans), F32, free), ((modes, chans), F32, free)],
        [vmem],
        [],
        8,
        100_000,
    )(gathered)

    gated, grad_proj = call(
        functools.partial(outputs_kernel, rows, steps, span, modes),
        "outputs",
        [((rows, chans), BF16, free), ((3, rows, chans), BF16, free)],
        [vmem] * 11 + [hbm] * 2,
        [
            pltpu.VMEM(pack_shape, F32),
            pltpu.VMEM(query_shape, F32),
            same_scratch,
            cum_scratch,
            pltpu.VMEM((ext_rows, LANES), BF16),
            pltpu.VMEM((chunk_rows, LANES), F32),
            coming_scratch,
            pltpu.VMEM((3, full_steps, SUB, LANES), F32),
            pltpu.VMEM((rows, rows), BF16),
            pltpu.VMEM((rows, 4 * LANES), F32),
            dma((tiles, 2)),
        ],
        16,
        40_000_000,
    )(
        *in_vmem(proj, cot),
        left,
        right,
        *in_vmem(taps_near, poles, keeps, order, picks),
        states,
        *in_vmem(feats),
        *in_hbm(pack, query),
    )
    return (gated, grad_proj, grad_tap, grad_res)


def solution(mesh):
    placed = (
        P(None, "ctx", "tp"),
        P(None, None, "tp"),
        P(None, "tp"),
        P(None, "tp"),
        P(),
        P("ctx", "tp"),
    )
    return jax.shard_map(
        per_device,
        mesh=mesh,
        in_specs=placed,
        out_specs=(P("ctx", "tp"), P(None, "ctx", "tp"), P(None, None, "tp"), P(None, "tp")),
        check_vma=False,
    )
```

```python
import functools
import math

import jax
import jax.numpy as jnp
from jax import lax
from jax.experimental import pallas as pl
from jax.experimental.pallas import tpu as pltpu
from jax.sharding import PartitionSpec as P

F32 = jnp.float32
BF16 = jnp.bfloat16
SUB = 8
LANES = 128
HALO = 16
SUM_ROWS = 32
MAX_DOC = 4096


def shift(block, distance):
    count = lax.axis_size("ctx")
    route = [(i, i + distance) for i in range(count) if 0 <= i + distance < count]
    return lax.ppermute(block, "ctx", route)


def spread(line):
    return jnp.broadcast_to(line, (SUB, LANES))


def power(base, exponent):
    for _ in range(int(math.log2(exponent))):
        base = base * base
    return base


def total_of(terms):
    terms = list(terms)
    while len(terms) > 1:
        terms = [a + b for a, b in zip(terms[::2], terms[1::2])] + terms[len(terms) & ~1 :]
    return terms[0]


def doc_ends(lens_ref):
    ends, total = [], jnp.int32(0)
    for d in range(lens_ref.shape[0]):
        total = total + lens_ref[d]
        ends.append(total)
    return ends


def keep_at(token, ends):
    starts = token == 0
    for end in ends:
        starts = jnp.logical_or(starts, token == end)
    return jnp.where(starts, 0.0, 1.0)


def fill_keep(keep_ref, ends, start, steps, span):
    token = lax.broadcasted_iota(jnp.int32, (SUB, LANES), 0) * steps + start
    for r in range(-span, steps + span):
        keep_ref[r + span] = keep_at(token + r, ends)


def fill_same(same_ref, keep_ref, span):
    for r in range(same_ref.shape[1]):
        running = keep_ref[r + span]
        same_ref[0, r] = running
        for j in range(2, span + 1):
            running = running * keep_ref[r + span - j + 1]
            same_ref[j - 1, r] = running


def fill_cum(cum_ref, keep_ref, steps, span):
    running = jnp.ones((SUB, LANES), F32)
    for r in range(steps):
        running = running * keep_ref[r + span]
        cum_ref[0, r] = running
    running = jnp.ones((SUB, LANES), F32)
    for r in range(steps - 1, -1, -1):
        running = running * keep_ref[r + 1 + span]
        cum_ref[1, r] = running


def fill_pick(pick_ref, ends, start, rows):
    shards = pick_ref.shape[1]
    last_start, next_start = jnp.int32(0), jnp.int32(shards * rows)
    for end in ends:
        last_start = jnp.where(end < start, jnp.maximum(last_start, end), last_start)
        next_start = jnp.where(end > start + rows, jnp.minimum(next_start, end), next_start)
    owner = lax.broadcasted_iota(jnp.int32, pick_ref.shape[1:], 0) * rows
    pick_ref[0] = jnp.where(owner + rows > last_start, 1.0, 0.0)
    pick_ref[1] = jnp.where(owner < next_start, 1.0, 0.0)


def fill_order(order_ref, steps):
    at = lax.broadcasted_iota(jnp.int32, order_ref.shape, 0)
    col = lax.broadcasted_iota(jnp.int32, order_ref.shape, 1)
    order_ref[...] = jnp.where((at & (SUB - 1)) * steps + (at >> 3) == col, 1.0, 0.0).astype(BF16)


def fill_rim_masks(mask_ref, ends, start, rows, span):
    last_start, next_start = jnp.int32(0), jnp.int32(1 << 30)
    for end in ends:
        last_start = jnp.where(end < start + rows, jnp.maximum(last_start, end), last_start)
        next_start = jnp.where(end > start, jnp.minimum(next_start, end), next_start)
    sub = lax.broadcasted_iota(jnp.int32, (SUB, LANES), 0)
    token = start + sub
    running = jnp.ones((SUB, LANES), F32)
    for j in range(span):
        running = running * keep_at(token - j, ends)
        mask_ref[j] = running
    mask_ref[span] = jnp.where(jnp.logical_and(sub < span, token >= last_start), 1.0, 0.0)
    mask_ref[span + 1] = jnp.where(jnp.logical_and(sub < span, token < next_start), 1.0, 0.0)


def at_step(r):
    return pl.ds(r * SUB, SUB)


def lanes_of(i):
    return pl.ds(i * LANES, LANES)


def load_kernel(
    steps, span,
    lens_hbm, proj_hbm, cot_hbm, taps_hbm, pole_hbm, res_hbm,
    left_ref, proj_ref, cot_ref, taps_ref, pole_ref, res_ref, keep_ref, rim_mask_ref, pick_ref, order_ref,
    lens_ref, small_sem, tile_sem,
):
    tiles, _, rows, _ = proj_ref.shape
    lens_copy = pltpu.make_async_copy(lens_hbm, lens_ref, small_sem.at[0])
    copies = [
        pltpu.make_async_copy(proj_hbm.at[:, pl.ds(rows - HALO, HALO), :], left_ref, small_sem.at[4]),
        pltpu.make_async_copy(taps_hbm, taps_ref, small_sem.at[1]),
        pltpu.make_async_copy(pole_hbm, pole_ref, small_sem.at[2]),
        pltpu.make_async_copy(res_hbm, res_ref, small_sem.at[3]),
    ]
    for n in range(tiles):
        at = lanes_of(n)
        copies.append(pltpu.make_async_copy(proj_hbm.at[:, :, at], proj_ref.at[n], tile_sem.at[n, 0]))
        copies.append(pltpu.make_async_copy(cot_hbm.at[:, at], cot_ref.at[n], tile_sem.at[n, 1]))
    lens_copy.start()
    for copy in copies:
        copy.start()
    fill_order(order_ref, steps)
    lens_copy.wait()
    start = lax.axis_index("ctx") * rows
    ends = doc_ends(lens_ref)
    fill_keep(keep_ref, ends, start, steps, span)
    fill_rim_masks(rim_mask_ref, ends, start, rows, span)
    fill_pick(pick_ref, ends, start, rows)
    for copy in copies:
        copy.wait()


def fir_steps(span, first, last, value_at, same_ref, taps):
    windows = [[value_at(i, first - 1 - j) for j in range(span)] for i in range(len(taps))]
    for r in range(first, last):
        same = [same_ref[j - 1, r] for j in range(1, span + 1)]
        results = []
        for i, stream_taps in enumerate(taps):
            windows[i] = [value_at(i, r)] + windows[i][:span]
            terms = [stream_taps[j] * (same[j - 1] * windows[i][j]) for j in range(1, span + 1)]
            results.append(total_of([stream_taps[0] * windows[i][0]] + terms))
        yield r, results


def fill_chunks(chunk_ref, tokens_ref, n, left_ref, streams, steps, span):
    sub = lax.broadcasted_iota(jnp.int32, (SUB, LANES), 0)
    lane_at = pl.ds(pl.multiple_of(n * LANES, LANES), LANES)
    for place, i in enumerate(streams):
        values = []
        for r in range(0, steps, 2):
            pair = tokens_ref[n, pl.ds(r * SUB, 2 * SUB), lanes_of(i)].astype(F32)
            values += [pair[:SUB], pair[SUB:]]
        for r in range(steps):
            chunk_ref[place, r + span] = values[r]
        for r in range(span if i < 3 else 0):
            halo = spread(left_ref[i, pl.ds(SUB - span + r, 1), lane_at])
            chunk_ref[place, r] = jnp.where(sub == 0, halo, pltpu.roll(values[steps - span + r], 1, 0))


def edges_kernel(
    steps, span, modes,
    proj_ref, cot_ref, taps_ref, pole_ref, keep_ref, order_ref,
    edge_ref, rim_ref, tokens_ref,
    same_ref, mask_ref, ext_ref, chunk_ref, feat_ref,
):
    tiles, _, rows, _ = proj_ref.shape
    fill_same(same_ref, keep_ref, span)
    sub = lax.broadcasted_iota(jnp.int32, (SUB, LANES), 0)
    running = jnp.ones((SUB, LANES), F32)
    ahead = jnp.where(sub == 0, 0.0, 1.0)
    for r in range(steps - 1, -1, -1):
        mask_ref[0, r] = running if r >= span else ahead * running
        running = running * keep_ref[r + span]
    through = [running]
    running = jnp.ones((SUB, LANES), F32)
    for r in range(steps):
        mask_ref[1, r] = running if r >= span else ahead * running
        running = running * keep_ref[r + 1 + span]
    through.append(running)

    def tile_step(n, carry):
        for i in range(4):
            ext_ref[:, lanes_of(i)] = proj_ref[n, i] if i < 3 else cot_ref[n]
        chunk_ref[...] = jnp.dot(order_ref[...], ext_ref[...], preferred_element_type=F32)
        tokens_ref[n] = chunk_ref[...].astype(BF16)
        for i in range(4):
            rim_ref[n, i] = ext_ref[pl.ds(0, HALO), lanes_of(i)].astype(F32)[:SUB]

        def chunk(i, r):
            value = chunk_ref[at_step(r % steps), lanes_of(i)]
            return value if r >= 0 else pltpu.roll(value, 1, 0)

        lane_at = pl.ds(pl.multiple_of(n * LANES, LANES), LANES)
        taps = [[spread(taps_ref[i, pl.ds(j, 1), lane_at]) for j in range(span + 1)] for i in range(3)]
        for r, (query, key, value) in fir_steps(span, 0, steps, chunk, same_ref, taps):
            feat_ref[0, r] = key * value * mask_ref[0, r]
            feat_ref[1, r] = query * chunk(3, r) * mask_ref[1, r]

        poles = [spread(pole_ref[pl.ds(m, 1), lane_at]) for m in range(modes)]
        for way in range(2):
            state = [jnp.zeros((SUB, LANES), F32)] * modes
            for r in range(steps) if way == 0 else range(steps - 1, -1, -1):
                source = feat_ref[way, r]
                state = [poles[m] * state[m] + source for m in range(modes)]
            open_ = through[way]
            factors = [power(poles[m], steps) for m in range(modes)]
            for hop in (1, 2, 4):
                move = hop if way == 0 else SUB - hop
                for m in range(modes):
                    state[m] = state[m] + (factors[m] * open_) * pltpu.roll(state[m], move, 0)
                    factors[m] = factors[m] * factors[m]
                open_ = open_ * pltpu.roll(open_, move, 0)
            last = SUB - 1 if way == 0 else 0
            for m in range(modes):
                edge_ref[way, pl.ds(m, 1), lane_at] = state[m][last : last + 1]
        return carry

    lax.fori_loop(0, tiles, tile_step, 0)


def rims_kernel(
    rows, span, modes,
    edge_ref, rim_ref, taps_ref, pole_ref, mask_ref, left_ref,
    send_ref, left_out_ref,
    ext_ref, line_ref, out_ref,
):
    tiles = rim_ref.shape[0]
    for n in range(tiles):
        at = lanes_of(n)
        made = []
        for i in range(3):
            left_out_ref[i, :, at] = left_ref[i, :, at].astype(F32)[HALO - SUB :]
            ext_ref[i, pl.ds(0, SUB)] = left_out_ref[i, :, at]
            ext_ref[i, pl.ds(SUB, SUB)] = rim_ref[n, i]
            value = spread(taps_ref[i, pl.ds(0, 1), at]) * rim_ref[n, i]
            for j in range(1, span + 1):
                value = value + spread(taps_ref[i, pl.ds(j, 1), at]) * (mask_ref[j - 1] * ext_ref[i, pl.ds(SUB - j, SUB)])
            made.append(value)
        line_ref[n, 0] = made[1] * made[2] * mask_ref[span]
        line_ref[n, 1] = made[0] * rim_ref[n, 3] * mask_ref[span + 1]
        pole = pole_ref[:, at]
        scale, bit, left_over = jnp.ones((modes, LANES), F32), pole, rows - span
        while left_over:
            if left_over & 1:
                scale = scale * bit
            bit = bit * bit
            left_over >>= 1
        for way in range(2):
            running = jnp.zeros((modes, LANES), F32)
            for t in range(span) if way == 0 else range(span - 1, -1, -1):
                running = running * pole + spread(line_ref[n, way, pl.ds(t, 1), :])
            out_ref[way, :, at] = edge_ref[way, :, at] + (scale * running if way == 0 else running)
    half = out_ref.shape[2] // 2
    ahead, behind = (
        jnp.concatenate([out_ref[way, :, pl.ds(0, half)], out_ref[way, :, pl.ds(half, half)]], axis=0).astype(BF16)
        for way in range(2)
    )
    me = lax.axis_index("ctx")

    def fill(value):
        def one(d, carry):
            send_ref[d] = value
            return carry

        return one

    lax.fori_loop(0, me, fill(behind), 0)
    lax.fori_loop(me, send_ref.shape[0], fill(ahead), 0)


def local_kernel(
    steps, span, modes,
    tokens_ref, left_ref, taps_ref, pole_ref, res_ref, keep_ref,
    feat_ref, sums_ref, pack_first_ref, pack_hbm, query_hbm,
    same_ref, chunk_ref, coef_ref, pack_ref, query_ref, out_sem,
):
    tiles = tokens_ref.shape[0]
    fill_same(same_ref, keep_ref, span)
    sub = lax.broadcasted_iota(jnp.int32, (SUB, LANES), 0)

    def run(first, count):
        running = keep_ref[first + span]
        for r in range(first + 1, first + count):
            running = running * keep_ref[r + span]
        return running

    through = [run(0, steps), run(1, steps)]
    onward = keep_ref[steps + span]

    def tile_results(n):
        return (
            pltpu.make_async_copy(pack_ref.at[n], pack_hbm.at[n], out_sem.at[n, 0]),
            pltpu.make_async_copy(query_ref.at[n], query_hbm.at[n], out_sem.at[n, 1]),
        )

    def tile_step(n, carry):
        lane_at = pl.ds(pl.multiple_of(n * LANES, LANES), LANES)
        fill_chunks(chunk_ref, tokens_ref, n, left_ref, range(4), steps, span)

        def chunk(i, r):
            return chunk_ref[i, r + span]

        taps = [[spread(taps_ref[i, pl.ds(j, 1), lane_at]) for j in range(span + 1)] for i in range(3)]
        for r, (query, key, value) in fir_steps(span, 0, steps, chunk, same_ref, taps):
            query_ref[n, r] = query
            feat_ref[n, 0, r] = key
            feat_ref[n, 1, r] = value

        pole_rows = pole_ref[:, lane_at]
        coef_ref[...] = res_ref[:, lane_at] * jnp.sqrt(1.0 - pole_rows * pole_rows)
        poles = [spread(pole_ref[pl.ds(m, 1), lane_at]) for m in range(modes)]
        coefs = [spread(coef_ref[pl.ds(m, 1), :]) for m in range(modes)]
        ends = []
        res_sums = [jnp.zeros((SUB, LANES), F32)] * modes
        for way in range(2):
            state = [jnp.zeros((SUB, LANES), F32)] * modes
            for r in range(steps) if way == 0 else range(steps - 1, -1, -1):
                if way == 0:
                    keep, source = keep_ref[r + span], feat_ref[n, 0, r] * feat_ref[n, 1, r]
                else:
                    keep, source = keep_ref[r + 1 + span], chunk(3, r) * query_ref[n, r]
                state = [(poles[m] * keep) * state[m] + source for m in range(modes)]
                pack_ref[n, way * steps + r] = total_of(coefs[m] * state[m] for m in range(modes))
                if way == 1:
                    carried = feat_ref[n, 0, r] * feat_ref[n, 1, r]
                    res_sums = [res_sums[m] + carried * state[m] for m in range(modes)]
            ends.append(state)

        for way in range(2):
            head = 0 if way == 0 else SUB - 1
            back = 1 if way == 0 else SUB - 1
            for m in range(modes):
                state = ends[way][m]
                factor = power(poles[m], steps)
                open_ = through[way]
                unit = factor * open_
                for hop in (1, 2, 4):
                    move = hop if way == 0 else SUB - hop
                    inside = sub >= hop if way == 0 else sub < SUB - hop
                    far = jnp.where(inside, pltpu.roll(state, move, 0), 0.0)
                    state = state + (factor * open_) * far
                    unit = unit * jnp.where(inside, pltpu.roll(unit, move, 0), 1.0)
                    open_ = open_ * jnp.where(inside, pltpu.roll(open_, move, 0), 1.0)
                    factor = factor * factor
                state = jnp.where(sub == head, 0.0, pltpu.roll(state, back, 0))
                unit = jnp.where(sub == head, 1.0, pltpu.roll(unit, back, 0))
                at = 2 * steps + way * 2 * modes + m
                pack_ref[n, at] = coefs[m] * state
                pack_ref[n, at + modes] = coefs[m] * unit
                if way == 1:
                    seen = poles[m] * onward * ends[0][m]
                    total = jnp.sum(res_sums[m] + seen * state, axis=0, keepdims=True)
                    sums_ref[0, pl.ds(m, 1), lane_at] = total
                    sums_ref[1, pl.ds(m, 1), lane_at] = jnp.sum(seen * unit, axis=0, keepdims=True)
        for copy in tile_results(n):
            copy.start()
        return carry

    lax.fori_loop(0, tiles, tile_step, 0)
    pack_first_ref[...] = pack_ref[0]
    for n in range(tiles):
        for copy in tile_results(n):
            copy.wait()


def fill_coming(coming_ref, states_ref, pick_ref, pole_ref, rows):
    shards = states_ref.shape[0]
    me = lax.axis_index("ctx")
    modes, chans = pole_ref.shape
    full = power(pole_ref[...], rows)
    half = chans // 2
    full = jnp.concatenate([full[:, :half], full[:, half:]], axis=0)
    weight = jnp.ones(full.shape, F32)
    totals = [jnp.zeros(full.shape, F32)] * 2
    for hop in range(1, min(shards - 1, -(-MAX_DOC // rows)) + 1):
        for way, j in enumerate((me - hop, me + hop)):
            inside = jnp.logical_and(j >= 0, j < shards).astype(F32)
            held = jnp.clip(j, 0, shards - 1)
            seen = jnp.broadcast_to(pick_ref[way, pl.ds(held, 1), :], full.shape) * inside
            totals[way] = totals[way] + (weight * seen) * states_ref[held].astype(F32)
        weight = weight * full
    for way, state in enumerate(totals):
        for n in range(chans // LANES):
            top, left = divmod(n * LANES, half)
            coming_ref[n, way] = state[top * modes : (top + 1) * modes, left : left + LANES]


def combine(way, n, steps, modes, pole_ref, pack_ref, coming_ref, cum_ref, lane_at):
    poles = [spread(pole_ref[pl.ds(m, 1), lane_at]) for m in range(modes)]
    at = 2 * steps + way * 2 * modes
    state = [
        pack_ref[n, at + m] + pack_ref[n, at + modes + m] * spread(coming_ref[n, way, pl.ds(m, 1), :])
        for m in range(modes)
    ]
    for r in range(steps) if way == 0 else range(steps - 1, -1, -1):
        state = [poles[m] * state[m] for m in range(modes)]
        yield r, pack_ref[n, way * steps + r] + cum_ref[way, r] * total_of(state)


def sums_kernel(
    rows, steps, span, modes,
    tokens_ref, left_ref, pole_ref, keep_ref, pick_ref, states_ref, feat_ref, res_ref, pack_first_ref, pack_hbm,
    out_ref, rim_ref,
    pack_ref, same_ref, cum_ref, chunk_ref, coming_ref, grad_ref, sums_ref, line_ref, tile_sem,
):
    tiles = feat_ref.shape[0]
    shards = states_ref.shape[0]

    def load(n):
        return pltpu.make_async_copy(pack_hbm.at[n], pack_ref.at[n], tile_sem.at[n])

    for n in range(1, tiles):
        load(n).start()
    pack_ref[0] = pack_first_ref[...]
    fill_same(same_ref, keep_ref, span)
    fill_cum(cum_ref, keep_ref, steps, span)
    sums_ref[...] = jnp.zeros_like(sums_ref)
    line_ref[...] = jnp.zeros_like(line_ref)
    fill_coming(coming_ref, states_ref, pick_ref, pole_ref, rows)
    scale = 1.0 / math.sqrt(shards * rows)

    def tile_step(n, carry):
        lane_at = pl.ds(pl.multiple_of(n * LANES, LANES), LANES)
        fill_chunks(chunk_ref, tokens_ref, n, left_ref, range(4), steps, span)

        @pl.when(n > 0)
        def _():
            load(n).wait()

        for way in range(2):
            for r, value in combine(way, n, steps, modes, pole_ref, pack_ref, coming_ref, cum_ref, lane_at):
                if way == 0:
                    grad_ref[0, r] = chunk_ref[3, r + span] * value
                else:
                    grad_ref[1, r] = value * feat_ref[n, 1, r]
                    grad_ref[2, r] = value * feat_ref[n, 0, r]
        for i in range(3):
            for r in range(span):
                line_ref[i, pl.ds(r, 1), lane_at] = grad_ref[i, r, pl.ds(0, 1), :]
        tap_sums = [[jnp.zeros((SUB, LANES), F32)] * (span + 1)] * 3
        windows = [[chunk_ref[i, span - 1 - j] for j in range(span)] for i in range(3)]
        for r in range(steps):
            same = [same_ref[j - 1, r] for j in range(1, span + 1)]
            for i in range(3):
                here = grad_ref[i, r]
                windows[i] = [chunk_ref[i, r + span]] + windows[i][:span]
                masked = [here] + [same[j] * here for j in range(span)]
                tap_sums[i] = [tap_sums[i][j] + masked[j] * windows[i][j] for j in range(span + 1)]
        for i in range(3):
            for j in range(span + 1):
                sums_ref[pl.ds((i * SUB + j) * SUB, SUB), lane_at] = tap_sums[i][j]
        return carry

    lax.fori_loop(0, tiles, tile_step, 0)
    rim_ref[...] = line_ref[...].astype(BF16)
    shape = (3 * SUB, 3 * SUB * SUB)
    at = lax.broadcasted_iota(jnp.int32, shape, 0)
    col = lax.broadcasted_iota(jnp.int32, shape, 1)
    gather = jnp.where((col >> 3) == at, 1.0, 0.0).astype(BF16)
    high = sums_ref[...].astype(BF16)
    low = (sums_ref[...] - high.astype(F32)).astype(BF16)
    taps = jnp.dot(gather, high, preferred_element_type=F32) + jnp.dot(gather, low, preferred_element_type=F32)
    pole = pole_ref[...]
    back = jnp.concatenate([coming_ref[n, 1] for n in range(tiles)], axis=1)
    res = (res_ref[0] + res_ref[1] * back) * jnp.sqrt(1.0 - pole * pole)
    out_ref[...] = (jnp.concatenate([taps, res], axis=0) * scale).astype(BF16)


def outputs_kernel(
    rows, steps, span, modes,
    tokens_ref, taps_ref, pole_ref, keep_ref, pick_ref, states_ref, feat_ref,
    pack_hbm, query_hbm,
    gated_ref, grad_proj_ref, tail_ref, tail_mask_ref,
    pack_ref, query_ref, same_ref, cum_ref, chunk_ref, coming_ref, grad_ref, back_ref, out_ref, tile_sem,
):
    tiles = feat_ref.shape[0]

    def loads(n):
        return (
            pltpu.make_async_copy(pack_hbm.at[n], pack_ref.at[n], tile_sem.at[n, 0]),
            pltpu.make_async_copy(query_hbm.at[n], query_ref.at[n], tile_sem.at[n, 1]),
        )

    for n in range(tiles):
        for copy in loads(n):
            copy.start()
    fill_same(same_ref, keep_ref, span)
    fill_cum(cum_ref, keep_ref, steps, span)
    at = lax.broadcasted_iota(jnp.int32, back_ref.shape, 0)
    col = lax.broadcasted_iota(jnp.int32, back_ref.shape, 1)
    sub = lax.broadcasted_iota(jnp.int32, (SUB, LANES), 0)
    back_ref[...] = jnp.where(at == (col & (SUB - 1)) * steps + (col >> 3), 1.0, 0.0).astype(BF16)
    fill_coming(coming_ref, states_ref, pick_ref, pole_ref, rows)

    def tile_step(n, carry):
        lane_at = pl.ds(pl.multiple_of(n * LANES, LANES), LANES)
        fill_chunks(chunk_ref, tokens_ref, n, None, (3,), steps, span)
        for copy in loads(n):
            copy.wait()
        for way in range(2):
            for r, value in combine(way, n, steps, modes, pole_ref, pack_ref, coming_ref, cum_ref, lane_at):
                if way == 0:
                    grad_ref[0, r] = chunk_ref[0, r + span] * value
                    out_ref[at_step(r), lanes_of(3)] = query_ref[n, r] * value
                else:
                    grad_ref[1, r] = value * feat_ref[n, 1, r]
                    grad_ref[2, r] = value * feat_ref[n, 0, r]
        for i in range(3):
            for r in range(span):
                grad_ref[i, steps + r] = jnp.where(sub == SUB - 1, 0.0, pltpu.roll(grad_ref[i, r], SUB - 1, 0))
        taps = [[spread(taps_ref[i, pl.ds(j, 1), lane_at]) for j in range(span + 1)] for i in range(3)]
        windows = [[grad_ref[i, r] for r in range(span)] for i in range(3)]
        for r in range(steps):
            same = [same_ref[j - 1, r + j] for j in range(1, span + 1)]
            for i in range(3):
                windows[i] = windows[i][-span:] + [grad_ref[i, r + span]]
                terms = [taps[i][j] * (same[j - 1] * windows[i][j]) for j in range(1, span + 1)]
                out_ref[at_step(r), lanes_of(i)] = total_of([taps[i][0] * windows[i][0]] + terms)
        for i in range(3):
            for r in range(steps - HALO, steps):
                last = out_ref[pl.ds(r * SUB + SUB - 1, 1), lanes_of(i)]
                tail_ref[i, pl.ds(r - steps + HALO, 1), lane_at] = last
        natural = jnp.dot(back_ref[...], out_ref[...].astype(BF16), preferred_element_type=F32).astype(BF16)
        gated_ref[:, lane_at] = natural[:, 3 * LANES :]
        for i in range(3):
            grad_proj_ref[i, :, lane_at] = natural[:, i * LANES : (i + 1) * LANES]
        return carry

    lax.fori_loop(0, tiles, tile_step, 0)
    for j in range(1, span + 1):
        for r in range(span):
            tail_mask_ref[j - 1, pl.ds(r, 1), :] = same_ref[j - 1, steps + r, pl.ds(SUB - 1, 1), :]


def tail_kernel(rows, span, partial_hbm, tail_ref, rim_ref, taps_ref, mask_ref, grad_proj_hbm, line_ref, sem):
    sub = lax.broadcasted_iota(jnp.int32, (SUB, LANES), 0)
    for n in range(rim_ref.shape[2] // LANES):
        at = lanes_of(n)
        for i in range(3):
            behind = rim_ref[i, :, at].astype(F32)[:SUB]
            value = tail_ref[i, pl.ds(HALO - SUB, SUB), at]
            for j in range(1, span + 1):
                added = spread(taps_ref[i, pl.ds(j, 1), at]) * (mask_ref[j - 1] * behind)
                value = value + pltpu.roll(jnp.where(sub < j, added, 0.0), SUB - j, 0)
            whole = jnp.concatenate([tail_ref[i, pl.ds(0, HALO - SUB), at], value], axis=0)
            line_ref[i, :, at] = whole.astype(BF16)
    copy = pltpu.make_async_copy(line_ref, grad_proj_hbm.at[:, pl.ds(rows - HALO, HALO), :], sem)
    copy.start()
    copy.wait()


def spread_kernel(one_ref, two_ref, three_ref, own_ref, out_ref):
    own, one, two, three = (ref[...].astype(F32) for ref in (own_ref, one_ref, two_ref, three_ref))
    total = ((own + two) + (one + three)).astype(BF16)
    for g in range(out_ref.shape[0]):
        out_ref[g] = total


def final_kernel(parts_ref, tap_ref, res_ref):
    total = total_of(parts_ref[g].astype(F32) for g in range(parts_ref.shape[0]))
    for i in range(3):
        tap_ref[i] = total[i * SUB : i * SUB + tap_ref.shape[1]]
    res_ref[...] = total[3 * SUB :]


def per_device(projected, short_taps, pole_decay, residues, doc_lengths, cotangent):
    rows, chans = projected.shape[1:]
    taps = short_taps.shape[1]
    span = taps - 1
    modes = pole_decay.shape[0]
    docs = doc_lengths.shape[0]
    shards = lax.axis_size("ctx")
    steps = rows // SUB
    tiles = chans // LANES
    full_steps = steps + span
    pack_shape = (tiles, 2 * steps + 4 * modes, SUB, LANES)
    query_shape = (tiles, steps, SUB, LANES)

    vmem = pl.BlockSpec(memory_space=pltpu.VMEM)
    hbm = pl.BlockSpec(memory_space=pltpu.HBM)
    free = jax.ShapeDtypeStruct
    dma = pltpu.SemaphoreType.DMA

    def in_hbm(*arrays):
        return [pltpu.with_memory_space_constraint(a, pltpu.HBM) for a in arrays]

    def in_vmem(*arrays):
        return [pltpu.with_memory_space_constraint(a, pltpu.VMEM) for a in arrays]

    def call(kernel, name, out_shape, in_specs, scratch, limit, flops, aliases=None):
        return pl.pallas_call(
            kernel,
            out_shape=tuple(space(shape, kind) for shape, kind, space in out_shape),
            in_specs=in_specs,
            out_specs=tuple(hbm if o[2] is pltpu.HBM else vmem for o in out_shape),
            scratch_shapes=scratch,
            input_output_aliases=aliases or {},
            compiler_params=pltpu.CompilerParams(vmem_limit_bytes=limit << 20),
            cost_estimate=pl.CostEstimate(flops=flops, bytes_accessed=4 << 20, transcendentals=0),
            name=name,
        )

    same_scratch = pltpu.VMEM((span, steps, SUB, LANES), F32)
    cum_scratch = pltpu.VMEM((2, steps, SUB, LANES), F32)
    chunk_scratch = pltpu.VMEM((4, full_steps, SUB, LANES), F32)
    coming_scratch = pltpu.VMEM((tiles, 2, modes, LANES), F32)

    left, proj, cot, taps_near, poles, weights, keeps, rim_masks, picks, order = call(
        functools.partial(load_kernel, steps, span),
        "load",
        [
            ((3, HALO, chans), BF16, free),
            ((tiles, 3, rows, LANES), BF16, pltpu.VMEM),
            ((tiles, rows, LANES), BF16, pltpu.VMEM),
            ((3, taps, chans), F32, pltpu.VMEM),
            ((modes, chans), F32, pltpu.VMEM),
            ((modes, chans), F32, pltpu.VMEM),
            ((full_steps + span, SUB, LANES), F32, pltpu.VMEM),
            ((taps + 1, SUB, LANES), F32, pltpu.VMEM),
            ((2, shards, chans // 2), F32, pltpu.VMEM),
            ((rows, rows), BF16, pltpu.VMEM),
        ],
        [hbm] * 6,
        [pltpu.SMEM((docs,), jnp.int32), dma((5,)), dma((tiles, 2))],
        8,
        1_000_000,
    )(*in_hbm(doc_lengths, projected, cotangent, short_taps, pole_decay, residues))
    left = shift(left, 1)

    edges, rims, tokens = call(
        functools.partial(edges_kernel, steps, span, modes),
        "edges",
        [
            ((2, modes, chans), F32, pltpu.VMEM),
            ((tiles, 4, SUB, LANES), F32, pltpu.VMEM),
            ((tiles, rows, 4 * LANES), BF16, pltpu.VMEM),
        ],
        [vmem] * 6,
        [
            same_scratch,
            pltpu.VMEM((2, steps, SUB, LANES), F32),
            pltpu.VMEM((rows, 4 * LANES), BF16),
            pltpu.VMEM((rows, 4 * LANES), F32),
            pltpu.VMEM((2, steps, SUB, LANES), F32),
        ],
        12,
        40_000_000,
    )(*in_vmem(proj, cot, taps_near, poles, keeps, order))

    outgoing, left = call(
        functools.partial(rims_kernel, rows, span, modes),
        "rims",
        [
            ((shards, 2 * modes, chans // 2), BF16, pltpu.VMEM),
            ((3, SUB, chans), F32, pltpu.VMEM),
        ],
        [vmem] * 6,
        [
            pltpu.VMEM((3, 2 * SUB, LANES), F32),
            pltpu.VMEM((tiles, 2, SUB, LANES), F32),
            pltpu.VMEM((2, modes, chans), F32),
        ],
        8,
        1_000_000,
    )(*in_vmem(edges, rims, taps_near, poles, rim_masks), left)

    states = lax.all_to_all(outgoing, "ctx", split_axis=0, concat_axis=0, tiled=True)

    feats, res_sums, pack_first, pack, query = call(
        functools.partial(local_kernel, steps, span, modes),
        "local",
        [
            ((tiles, 2, steps, SUB, LANES), F32, pltpu.VMEM),
            ((2, modes, chans), F32, pltpu.VMEM),
            (pack_shape[1:], F32, pltpu.VMEM),
            (pack_shape, F32, pltpu.HBM),
            (query_shape, F32, pltpu.HBM),
        ],
        [vmem] * 6,
        [
            same_scratch,
            chunk_scratch,
            pltpu.VMEM((modes, LANES), F32),
            pltpu.VMEM(pack_shape, F32),
            pltpu.VMEM(query_shape, F32),
            dma((tiles, 2)),
        ],
        16,
        60_000_000,
    )(*in_vmem(tokens, left, taps_near, poles, weights, keeps))

    sums, ahead = call(
        functools.partial(sums_kernel, rows, steps, span, modes),
        "sums",
        [((SUM_ROWS, chans), BF16, free), ((3, HALO, chans), BF16, free)],
        [vmem] * 9 + [hbm],
        [
            pltpu.VMEM(pack_shape, F32),
            same_scratch,
            cum_scratch,
            chunk_scratch,
            coming_scratch,
            pltpu.VMEM((3, steps, SUB, LANES), F32),
            pltpu.VMEM((3 * SUB * SUB, chans), F32),
            pltpu.VMEM((3, HALO, chans), F32),
            dma((tiles,)),
        ],
        12,
        30_000_000,
    )(
        *in_vmem(tokens, left, poles, keeps, picks),
        states,
        *in_vmem(feats, res_sums, pack_first),
        *in_hbm(pack),
    )

    behind = shift(ahead, -1)

    near = 4
    far = shards // near

    def around(block, hop):
        return lax.ppermute(
            block, "ctx", [(i, i // near * near + (i + hop) % near) for i in range(shards)]
        )

    (parts,) = call(
        spread_kernel, "spread", [((far, SUM_ROWS, chans), BF16, pltpu.VMEM)], [vmem] * 4, [], 4, 100_000
    )(*(around(sums, hop) for hop in (1, 2, 3)), sums)
    groups = [[f * near + n for f in range(far)] for n in range(near)]
    gathered = lax.all_to_all(parts, "ctx", 0, 0, tiled=True, axis_index_groups=groups)
    grad_tap, grad_res = call(
        final_kernel,
        "final",
        [((3, taps, chans), F32, free), ((modes, chans), F32, free)],
        [vmem],
        [],
        8,
        100_000,
    )(gathered)

    gated, grad_proj, tail, tail_mask = call(
        functools.partial(outputs_kernel, rows, steps, span, modes),
        "outputs",
        [
            ((rows, chans), BF16, free),
            ((3, rows, chans), BF16, free),
            ((3, HALO, chans), F32, pltpu.VMEM),
            ((span, SUB, LANES), F32, pltpu.VMEM),
        ],
        [vmem] * 7 + [hbm] * 2,
        [
            pltpu.VMEM(pack_shape, F32),
            pltpu.VMEM(query_shape, F32),
            pltpu.VMEM((span, full_steps, SUB, LANES), F32),
            cum_scratch,
            pltpu.VMEM((1, full_steps, SUB, LANES), F32),
            coming_scratch,
            pltpu.VMEM((3, full_steps, SUB, LANES), F32),
            pltpu.VMEM((rows, rows), BF16),
            pltpu.VMEM((rows, 4 * LANES), F32),
            dma((tiles, 2)),
        ],
        16,
        40_000_000,
    )(
        *in_vmem(tokens, taps_near, poles, keeps, picks),
        states,
        *in_vmem(feats),
        *in_hbm(pack, query),
    )
    (grad_proj,) = call(
        functools.partial(tail_kernel, rows, span),
        "tail",
        [((3, rows, chans), BF16, pltpu.HBM)],
        [hbm] + [vmem] * 4,
        [pltpu.VMEM((3, HALO, chans), BF16), dma],
        4,
        500_000,
        aliases={0: 0},
    )(*in_hbm(grad_proj), *in_vmem(tail), behind, *in_vmem(taps_near, tail_mask))
    return (gated, grad_proj, grad_tap, grad_res)


def solution(mesh):
    placed = (
        P(None, "ctx", "tp"),
        P(None, None, "tp"),
        P(None, "tp"),
        P(None, "tp"),
        P(),
        P("ctx", "tp"),
    )
    return jax.shard_map(
        per_device,
        mesh=mesh,
        in_specs=placed,
        out_specs=(P("ctx", "tp"), P(None, "ctx", "tp"), P(None, None, "tp"), P(None, "tp")),
        check_vma=False,
    )
```

```python
import functools
import math

import jax
import jax.numpy as jnp
from jax import lax
from jax.experimental import pallas as pl
from jax.experimental.pallas import tpu as pltpu
from jax.sharding import PartitionSpec as P

F32 = jnp.float32
BF16 = jnp.bfloat16
SUB = 8
LANES = 128
HALO = 16
SUM_ROWS = 32
MAX_DOC = 4096


def shift(block, distance):
    count = lax.axis_size("ctx")
    route = [(i, i + distance) for i in range(count) if 0 <= i + distance < count]
    return lax.ppermute(block, "ctx", route)


def spread(line):
    return jnp.broadcast_to(line, (SUB, LANES))


def power(base, exponent):
    for _ in range(int(math.log2(exponent))):
        base = base * base
    return base


def total_of(terms):
    terms = list(terms)
    while len(terms) > 1:
        terms = [a + b for a, b in zip(terms[::2], terms[1::2])] + terms[len(terms) & ~1 :]
    return terms[0]


def doc_ends(lens_ref):
    ends, total = [], jnp.int32(0)
    for d in range(lens_ref.shape[0]):
        total = total + lens_ref[d]
        ends.append(total)
    return ends


def keep_at(token, ends):
    starts = token == 0
    for end in ends:
        starts = jnp.logical_or(starts, token == end)
    return jnp.where(starts, 0.0, 1.0)


def fill_keep(keep_ref, ends, start, steps, span):
    token = lax.broadcasted_iota(jnp.int32, (SUB, LANES), 0) * steps + start
    for r in range(-span, steps + span):
        keep_ref[r + span] = keep_at(token + r, ends)


def fill_same(same_ref, keep_ref, span):
    for r in range(same_ref.shape[1]):
        running = keep_ref[r + span]
        same_ref[0, r] = running
        for j in range(2, span + 1):
            running = running * keep_ref[r + span - j + 1]
            same_ref[j - 1, r] = running


def fill_cum(cum_ref, keep_ref, steps, span):
    running = jnp.ones((SUB, LANES), F32)
    for r in range(steps):
        running = running * keep_ref[r + span]
        cum_ref[0, r] = running
    running = jnp.ones((SUB, LANES), F32)
    for r in range(steps - 1, -1, -1):
        running = running * keep_ref[r + 1 + span]
        cum_ref[1, r] = running


def fill_pick(pick_ref, ends, start, rows):
    shards = pick_ref.shape[1]
    last_start, next_start = jnp.int32(0), jnp.int32(shards * rows)
    for end in ends:
        last_start = jnp.where(end < start, jnp.maximum(last_start, end), last_start)
        next_start = jnp.where(end > start + rows, jnp.minimum(next_start, end), next_start)
    owner = lax.broadcasted_iota(jnp.int32, pick_ref.shape[1:], 0) * rows
    pick_ref[0] = jnp.where(owner + rows > last_start, 1.0, 0.0)
    pick_ref[1] = jnp.where(owner < next_start, 1.0, 0.0)


def fill_rim_masks(mask_ref, ends, start, rows, span):
    last_start, next_start = jnp.int32(0), jnp.int32(1 << 30)
    for end in ends:
        last_start = jnp.where(end < start + rows, jnp.maximum(last_start, end), last_start)
        next_start = jnp.where(end > start, jnp.minimum(next_start, end), next_start)
    sub = lax.broadcasted_iota(jnp.int32, (SUB, LANES), 0)
    token = start + sub
    running = jnp.ones((SUB, LANES), F32)
    for j in range(span):
        running = running * keep_at(token - j, ends)
        mask_ref[j] = running
    mask_ref[span] = jnp.where(jnp.logical_and(sub < span, token >= last_start), 1.0, 0.0)
    mask_ref[span + 1] = jnp.where(jnp.logical_and(sub < span, token < next_start), 1.0, 0.0)


def at_step(r):
    return pl.ds(r * SUB, SUB)


def lanes_of(i):
    return pl.ds(i * LANES, LANES)


def load_kernel(
    steps, span,
    lens_hbm, proj_hbm, cot_hbm, taps_hbm, pole_hbm, res_hbm,
    left_ref, proj_ref, cot_ref, taps_ref, pole_ref, res_ref, keep_ref, rim_mask_ref, pick_ref,
    lens_ref, small_sem, tile_sem,
):
    tiles, _, rows, _ = proj_ref.shape
    lens_copy = pltpu.make_async_copy(lens_hbm, lens_ref, small_sem.at[0])
    copies = [
        pltpu.make_async_copy(proj_hbm.at[:, pl.ds(rows - HALO, HALO), :], left_ref, small_sem.at[4]),
        pltpu.make_async_copy(taps_hbm, taps_ref, small_sem.at[1]),
        pltpu.make_async_copy(pole_hbm, pole_ref, small_sem.at[2]),
        pltpu.make_async_copy(res_hbm, res_ref, small_sem.at[3]),
    ]
    for n in range(tiles):
        at = lanes_of(n)
        copies.append(pltpu.make_async_copy(proj_hbm.at[:, :, at], proj_ref.at[n], tile_sem.at[n, 0]))
        copies.append(pltpu.make_async_copy(cot_hbm.at[:, at], cot_ref.at[n], tile_sem.at[n, 1]))
    lens_copy.start()
    for copy in copies:
        copy.start()
    lens_copy.wait()
    start = lax.axis_index("ctx") * rows
    ends = doc_ends(lens_ref)
    fill_keep(keep_ref, ends, start, steps, span)
    fill_rim_masks(rim_mask_ref, ends, start, rows, span)
    fill_pick(pick_ref, ends, start, rows)
    for copy in copies:
        copy.wait()


def fir_steps(span, first, last, value_at, same_ref, taps):
    windows = [[value_at(i, first - 1 - j) for j in range(span)] for i in range(len(taps))]
    for r in range(first, last):
        same = [same_ref[j - 1, r] for j in range(1, span + 1)]
        results = []
        for i, stream_taps in enumerate(taps):
            windows[i] = [value_at(i, r)] + windows[i][:span]
            terms = [stream_taps[j] * (same[j - 1] * windows[i][j]) for j in range(1, span + 1)]
            results.append(total_of([stream_taps[0] * windows[i][0]] + terms))
        yield r, results


def fill_chunks(chunk_ref, tokens_ref, n, left_ref, streams, steps, span):
    sub = lax.broadcasted_iota(jnp.int32, (SUB, LANES), 0)
    lane_at = pl.ds(pl.multiple_of(n * LANES, LANES), LANES)
    for place, i in enumerate(streams):
        values = []
        for r in range(0, steps, 2):
            pair = tokens_ref[n, pl.ds(r * SUB, 2 * SUB), lanes_of(i)].astype(F32)
            values += [pair[:SUB], pair[SUB:]]
        for r in range(steps):
            chunk_ref[place, r + span] = values[r]
        for r in range(span if i < 3 else 0):
            halo = spread(left_ref[i, pl.ds(SUB - span + r, 1), lane_at])
            chunk_ref[place, r] = jnp.where(sub == 0, halo, pltpu.roll(values[steps - span + r], 1, 0))


def edges_kernel(
    steps, span, modes,
    proj_ref, cot_ref, taps_ref, pole_ref, keep_ref,
    edge_ref, rim_ref, tokens_ref,
    same_ref, mask_ref, chunk_ref, feat_ref,
):
    tiles, _, rows, _ = proj_ref.shape
    fill_same(same_ref, keep_ref, span)
    sub = lax.broadcasted_iota(jnp.int32, (SUB, LANES), 0)
    running = jnp.ones((SUB, LANES), F32)
    ahead = jnp.where(sub == 0, 0.0, 1.0)
    for r in range(steps - 1, -1, -1):
        mask_ref[0, r] = running if r >= span else ahead * running
        running = running * keep_ref[r + span]
    through = [running]
    running = jnp.ones((SUB, LANES), F32)
    for r in range(steps):
        mask_ref[1, r] = running if r >= span else ahead * running
        running = running * keep_ref[r + 1 + span]
    through.append(running)

    def tile_step(n, carry):
        for i in range(4):
            natural = (proj_ref[n, i] if i < 3 else cot_ref[n]).astype(F32)
            rim_ref[n, i] = natural[:SUB]
            ordered = jnp.swapaxes(natural.reshape(SUB, steps, LANES), 0, 1)
            chunk_ref[i] = ordered
            tokens_ref[n, :, lanes_of(i)] = ordered.reshape(rows, LANES).astype(BF16)

        def chunk(i, r):
            value = chunk_ref[i, r % steps]
            return value if r >= 0 else pltpu.roll(value, 1, 0)

        lane_at = pl.ds(pl.multiple_of(n * LANES, LANES), LANES)
        taps = [[spread(taps_ref[i, pl.ds(j, 1), lane_at]) for j in range(span + 1)] for i in range(3)]
        for r, (query, key, value) in fir_steps(span, 0, steps, chunk, same_ref, taps):
            feat_ref[0, r] = key * value * mask_ref[0, r]
            feat_ref[1, r] = query * chunk(3, r) * mask_ref[1, r]

        poles = [spread(pole_ref[pl.ds(m, 1), lane_at]) for m in range(modes)]
        for way in range(2):
            state = [jnp.zeros((SUB, LANES), F32)] * modes
            for r in range(steps) if way == 0 else range(steps - 1, -1, -1):
                source = feat_ref[way, r]
                state = [poles[m] * state[m] + source for m in range(modes)]
            open_ = through[way]
            factors = [power(poles[m], steps) for m in range(modes)]
            for hop in (1, 2, 4):
                move = hop if way == 0 else SUB - hop
                for m in range(modes):
                    state[m] = state[m] + (factors[m] * open_) * pltpu.roll(state[m], move, 0)
                    factors[m] = factors[m] * factors[m]
                open_ = open_ * pltpu.roll(open_, move, 0)
            last = SUB - 1 if way == 0 else 0
            for m in range(modes):
                edge_ref[way, pl.ds(m, 1), lane_at] = state[m][last : last + 1]
        return carry

    lax.fori_loop(0, tiles, tile_step, 0, unroll=True)


def rims_kernel(
    rows, span, modes,
    edge_ref, rim_ref, taps_ref, pole_ref, mask_ref, left_ref,
    send_ref, left_out_ref,
    ext_ref, line_ref, out_ref,
):
    tiles = rim_ref.shape[0]
    for n in range(tiles):
        at = lanes_of(n)
        made = []
        for i in range(3):
            left_out_ref[i, :, at] = left_ref[i, :, at].astype(F32)[HALO - SUB :]
            ext_ref[i, pl.ds(0, SUB)] = left_out_ref[i, :, at]
            ext_ref[i, pl.ds(SUB, SUB)] = rim_ref[n, i]
            value = spread(taps_ref[i, pl.ds(0, 1), at]) * rim_ref[n, i]
            for j in range(1, span + 1):
                value = value + spread(taps_ref[i, pl.ds(j, 1), at]) * (mask_ref[j - 1] * ext_ref[i, pl.ds(SUB - j, SUB)])
            made.append(value)
        line_ref[n, 0] = made[1] * made[2] * mask_ref[span]
        line_ref[n, 1] = made[0] * rim_ref[n, 3] * mask_ref[span + 1]
        pole = pole_ref[:, at]
        scale, bit, left_over = jnp.ones((modes, LANES), F32), pole, rows - span
        while left_over:
            if left_over & 1:
                scale = scale * bit
            bit = bit * bit
            left_over >>= 1
        for way in range(2):
            running = jnp.zeros((modes, LANES), F32)
            for t in range(span) if way == 0 else range(span - 1, -1, -1):
                running = running * pole + spread(line_ref[n, way, pl.ds(t, 1), :])
            out_ref[way, :, at] = edge_ref[way, :, at] + (scale * running if way == 0 else running)
    half = out_ref.shape[2] // 2
    ahead, behind = (
        jnp.concatenate([out_ref[way, :, pl.ds(0, half)], out_ref[way, :, pl.ds(half, half)]], axis=0).astype(BF16)
        for way in range(2)
    )
    me = lax.axis_index("ctx")

    def fill(value):
        def one(d, carry):
            send_ref[d] = value
            return carry

        return one

    lax.fori_loop(0, me, fill(behind), 0)
    lax.fori_loop(me, send_ref.shape[0], fill(ahead), 0)


def local_kernel(
    steps, span, modes,
    tokens_ref, left_ref, taps_ref, pole_ref, res_ref, keep_ref,
    feat_ref, sums_ref, pack_first_ref, pack_hbm, query_hbm,
    same_ref, chunk_ref, coef_ref, pack_ref, query_ref, out_sem,
):
    tiles = tokens_ref.shape[0]
    fill_same(same_ref, keep_ref, span)
    sub = lax.broadcasted_iota(jnp.int32, (SUB, LANES), 0)

    def run(first, count):
        running = keep_ref[first + span]
        for r in range(first + 1, first + count):
            running = running * keep_ref[r + span]
        return running

    through = [run(0, steps), run(1, steps)]
    onward = keep_ref[steps + span]

    def tile_results(n):
        return (
            pltpu.make_async_copy(pack_ref.at[n], pack_hbm.at[n], out_sem.at[n, 0]),
            pltpu.make_async_copy(query_ref.at[n], query_hbm.at[n], out_sem.at[n, 1]),
        )

    def tile_step(n, carry):
        lane_at = pl.ds(pl.multiple_of(n * LANES, LANES), LANES)
        fill_chunks(chunk_ref, tokens_ref, n, left_ref, range(4), steps, span)

        def chunk(i, r):
            return chunk_ref[i, r + span]

        taps = [[spread(taps_ref[i, pl.ds(j, 1), lane_at]) for j in range(span + 1)] for i in range(3)]
        for r, (query, key, value) in fir_steps(span, 0, steps, chunk, same_ref, taps):
            query_ref[n, r] = query
            feat_ref[n, 0, r] = key
            feat_ref[n, 1, r] = value

        pole_rows = pole_ref[:, lane_at]
        coef_ref[...] = res_ref[:, lane_at] * jnp.sqrt(1.0 - pole_rows * pole_rows)
        poles = [spread(pole_ref[pl.ds(m, 1), lane_at]) for m in range(modes)]
        coefs = [spread(coef_ref[pl.ds(m, 1), :]) for m in range(modes)]
        ends = []
        res_sums = [jnp.zeros((SUB, LANES), F32)] * modes
        for way in range(2):
            state = [jnp.zeros((SUB, LANES), F32)] * modes
            for r in range(steps) if way == 0 else range(steps - 1, -1, -1):
                if way == 0:
                    keep, source = keep_ref[r + span], feat_ref[n, 0, r] * feat_ref[n, 1, r]
                else:
                    keep, source = keep_ref[r + 1 + span], chunk(3, r) * query_ref[n, r]
                state = [(poles[m] * keep) * state[m] + source for m in range(modes)]
                pack_ref[n, way * steps + r] = total_of(coefs[m] * state[m] for m in range(modes))
                if way == 1:
                    carried = feat_ref[n, 0, r] * feat_ref[n, 1, r]
                    res_sums = [res_sums[m] + carried * state[m] for m in range(modes)]
            ends.append(state)

        for way in range(2):
            head = 0 if way == 0 else SUB - 1
            back = 1 if way == 0 else SUB - 1
            for m in range(modes):
                state = ends[way][m]
                factor = power(poles[m], steps)
                open_ = through[way]
                unit = factor * open_
                for hop in (1, 2, 4):
                    move = hop if way == 0 else SUB - hop
                    inside = sub >= hop if way == 0 else sub < SUB - hop
                    far = jnp.where(inside, pltpu.roll(state, move, 0), 0.0)
                    state = state + (factor * open_) * far
                    unit = unit * jnp.where(inside, pltpu.roll(unit, move, 0), 1.0)
                    open_ = open_ * jnp.where(inside, pltpu.roll(open_, move, 0), 1.0)
                    factor = factor * factor
                state = jnp.where(sub == head, 0.0, pltpu.roll(state, back, 0))
                unit = jnp.where(sub == head, 1.0, pltpu.roll(unit, back, 0))
                at = 2 * steps + way * 2 * modes + m
                pack_ref[n, at] = coefs[m] * state
                pack_ref[n, at + modes] = coefs[m] * unit
                if way == 1:
                    seen = poles[m] * onward * ends[0][m]
                    total = jnp.sum(res_sums[m] + seen * state, axis=0, keepdims=True)
                    sums_ref[0, pl.ds(m, 1), lane_at] = total
                    sums_ref[1, pl.ds(m, 1), lane_at] = jnp.sum(seen * unit, axis=0, keepdims=True)
        for copy in tile_results(n):
            copy.start()
        return carry

    lax.fori_loop(0, tiles, tile_step, 0)
    pack_first_ref[...] = pack_ref[0]
    for n in range(tiles):
        for copy in tile_results(n):
            copy.wait()


def fill_coming(coming_ref, states_ref, pick_ref, pole_ref, rows):
    shards = states_ref.shape[0]
    me = lax.axis_index("ctx")
    modes, chans = pole_ref.shape
    full = power(pole_ref[...], rows)
    half = chans // 2
    full = jnp.concatenate([full[:, :half], full[:, half:]], axis=0)
    weight = jnp.ones(full.shape, F32)
    totals = [jnp.zeros(full.shape, F32)] * 2
    for hop in range(1, min(shards - 1, -(-MAX_DOC // rows)) + 1):
        for way, j in enumerate((me - hop, me + hop)):
            inside = jnp.logical_and(j >= 0, j < shards).astype(F32)
            held = jnp.clip(j, 0, shards - 1)
            seen = jnp.broadcast_to(pick_ref[way, pl.ds(held, 1), :], full.shape) * inside
            totals[way] = totals[way] + (weight * seen) * states_ref[held].astype(F32)
        weight = weight * full
    for way, state in enumerate(totals):
        for n in range(chans // LANES):
            top, left = divmod(n * LANES, half)
            coming_ref[n, way] = state[top * modes : (top + 1) * modes, left : left + LANES]


def combine(way, n, steps, modes, pole_ref, pack_ref, coming_ref, cum_ref, lane_at):
    poles = [spread(pole_ref[pl.ds(m, 1), lane_at]) for m in range(modes)]
    at = 2 * steps + way * 2 * modes
    state = [
        pack_ref[n, at + m] + pack_ref[n, at + modes + m] * spread(coming_ref[n, way, pl.ds(m, 1), :])
        for m in range(modes)
    ]
    for r in range(steps) if way == 0 else range(steps - 1, -1, -1):
        state = [poles[m] * state[m] for m in range(modes)]
        yield r, pack_ref[n, way * steps + r] + cum_ref[way, r] * total_of(state)


def sums_kernel(
    rows, steps, span, modes,
    tokens_ref, left_ref, pole_ref, keep_ref, pick_ref, states_ref, feat_ref, res_ref, pack_first_ref, pack_hbm,
    out_ref, rim_ref,
    pack_ref, same_ref, cum_ref, chunk_ref, coming_ref, grad_ref, sums_ref, line_ref, tile_sem,
):
    tiles = feat_ref.shape[0]
    shards = states_ref.shape[0]

    def load(n):
        return pltpu.make_async_copy(pack_hbm.at[n], pack_ref.at[n], tile_sem.at[n])

    for n in range(1, tiles):
        load(n).start()
    pack_ref[0] = pack_first_ref[...]
    fill_same(same_ref, keep_ref, span)
    fill_cum(cum_ref, keep_ref, steps, span)
    sums_ref[...] = jnp.zeros_like(sums_ref)
    line_ref[...] = jnp.zeros_like(line_ref)
    fill_coming(coming_ref, states_ref, pick_ref, pole_ref, rows)
    scale = 1.0 / math.sqrt(shards * rows)

    def tile_step(n, carry):
        lane_at = pl.ds(pl.multiple_of(n * LANES, LANES), LANES)
        fill_chunks(chunk_ref, tokens_ref, n, left_ref, range(4), steps, span)

        @pl.when(n > 0)
        def _():
            load(n).wait()

        for way in range(2):
            for r, value in combine(way, n, steps, modes, pole_ref, pack_ref, coming_ref, cum_ref, lane_at):
                if way == 0:
                    grad_ref[0, r] = chunk_ref[3, r + span] * value
                else:
                    grad_ref[1, r] = value * feat_ref[n, 1, r]
                    grad_ref[2, r] = value * feat_ref[n, 0, r]
        for i in range(3):
            for r in range(span):
                line_ref[i, pl.ds(r, 1), lane_at] = grad_ref[i, r, pl.ds(0, 1), :]
        tap_sums = [[jnp.zeros((SUB, LANES), F32)] * (span + 1)] * 3
        windows = [[chunk_ref[i, span - 1 - j] for j in range(span)] for i in range(3)]
        for r in range(steps):
            same = [same_ref[j - 1, r] for j in range(1, span + 1)]
            for i in range(3):
                here = grad_ref[i, r]
                windows[i] = [chunk_ref[i, r + span]] + windows[i][:span]
                masked = [here] + [same[j] * here for j in range(span)]
                tap_sums[i] = [tap_sums[i][j] + masked[j] * windows[i][j] for j in range(span + 1)]
        for i in range(3):
            for j in range(span + 1):
                sums_ref[pl.ds((i * SUB + j) * SUB, SUB), lane_at] = tap_sums[i][j]
        return carry

    lax.fori_loop(0, tiles, tile_step, 0)
    rim_ref[...] = line_ref[...].astype(BF16)
    shape = (3 * SUB, 3 * SUB * SUB)
    at = lax.broadcasted_iota(jnp.int32, shape, 0)
    col = lax.broadcasted_iota(jnp.int32, shape, 1)
    gather = jnp.where((col >> 3) == at, 1.0, 0.0).astype(BF16)
    high = sums_ref[...].astype(BF16)
    low = (sums_ref[...] - high.astype(F32)).astype(BF16)
    taps = jnp.dot(gather, high, preferred_element_type=F32) + jnp.dot(gather, low, preferred_element_type=F32)
    pole = pole_ref[...]
    back = jnp.concatenate([coming_ref[n, 1] for n in range(tiles)], axis=1)
    res = (res_ref[0] + res_ref[1] * back) * jnp.sqrt(1.0 - pole * pole)
    out_ref[...] = (jnp.concatenate([taps, res], axis=0) * scale).astype(BF16)


def outputs_kernel(
    rows, steps, span, modes,
    tokens_ref, taps_ref, pole_ref, keep_ref, pick_ref, states_ref, feat_ref, pack_first_ref,
    pack_hbm, query_hbm,
    gated_hbm, grad_proj_hbm, tail_ref, tail_mask_ref,
    pack_ref, query_ref, same_ref, cum_ref, chunk_ref, coming_ref, grad_ref, out_ref, gated_ref, grad_proj_ref,
    pack_sem, query_sem, out_sem,
):
    tiles = feat_ref.shape[0]

    def load_pack(n):
        return pltpu.make_async_copy(pack_hbm.at[n], pack_ref.at[n], pack_sem.at[n])

    def load_query(n):
        return pltpu.make_async_copy(query_hbm.at[n], query_ref.at[n], query_sem.at[n])

    def results(n):
        at = pl.ds(n * LANES, LANES)
        if not isinstance(n, int):
            at = pl.ds(pl.multiple_of(n * LANES, LANES), LANES)
        return (
            pltpu.make_async_copy(gated_ref.at[n], gated_hbm.at[:, at], out_sem.at[n, 0]),
            pltpu.make_async_copy(grad_proj_ref.at[n], grad_proj_hbm.at[:, :, at], out_sem.at[n, 1]),
        )

    for n in range(tiles):
        load_query(n).start()
        if n > 0:
            load_pack(n).start()
    pack_ref[0] = pack_first_ref[...]
    fill_same(same_ref, keep_ref, span)
    fill_cum(cum_ref, keep_ref, steps, span)
    sub = lax.broadcasted_iota(jnp.int32, (SUB, LANES), 0)
    fill_coming(coming_ref, states_ref, pick_ref, pole_ref, rows)

    def tile_step(n, carry):
        lane_at = pl.ds(pl.multiple_of(n * LANES, LANES), LANES)
        fill_chunks(chunk_ref, tokens_ref, n, None, (3,), steps, span)

        @pl.when(n > 0)
        def _():
            load_pack(n).wait()

        for way in range(2):
            for r, value in combine(way, n, steps, modes, pole_ref, pack_ref, coming_ref, cum_ref, lane_at):
                if way == 0:
                    grad_ref[0, r] = chunk_ref[0, r + span] * value
                    out_ref[3, r] = value
                else:
                    grad_ref[1, r] = value * feat_ref[n, 1, r]
                    grad_ref[2, r] = value * feat_ref[n, 0, r]
        for i in range(3):
            for r in range(span):
                grad_ref[i, steps + r] = jnp.where(sub == SUB - 1, 0.0, pltpu.roll(grad_ref[i, r], SUB - 1, 0))
        taps = [[spread(taps_ref[i, pl.ds(j, 1), lane_at]) for j in range(span + 1)] for i in range(3)]
        windows = [[grad_ref[i, r] for r in range(span)] for i in range(3)]
        for r in range(steps):
            same = [same_ref[j - 1, r + j] for j in range(1, span + 1)]
            for i in range(3):
                windows[i] = windows[i][-span:] + [grad_ref[i, r + span]]
                terms = [taps[i][j] * (same[j - 1] * windows[i][j]) for j in range(1, span + 1)]
                out_ref[i, r] = total_of([taps[i][0] * windows[i][0]] + terms)
        gated_copy, grad_copy = results(n)
        for i in range(3):
            natural = jnp.swapaxes(out_ref[i], 0, 1).reshape(SUB * steps, LANES)
            tail_ref[i, :, lane_at] = natural[SUB * steps - HALO :]
            grad_proj_ref[n, i] = natural.astype(BF16)
        grad_copy.start()
        load_query(n).wait()
        gated_ref[n] = jnp.swapaxes(query_ref[n] * out_ref[3], 0, 1).reshape(SUB * steps, LANES).astype(BF16)
        gated_copy.start()
        return carry

    lax.fori_loop(0, tiles, tile_step, 0)
    for n in range(tiles):
        for copy in results(n):
            copy.wait()
    for j in range(1, span + 1):
        for r in range(span):
            tail_mask_ref[j - 1, pl.ds(r, 1), :] = same_ref[j - 1, steps + r, pl.ds(SUB - 1, 1), :]


def spread_kernel(one_ref, two_ref, three_ref, own_ref, out_ref):
    own, one, two, three = (ref[...].astype(F32) for ref in (own_ref, one_ref, two_ref, three_ref))
    total = ((own + two) + (one + three)).astype(BF16)
    for g in range(out_ref.shape[0]):
        out_ref[g] = total


def final_kernel(
    rows, span, partial_hbm, parts_ref, tail_ref, rim_ref, taps_ref, mask_ref,
    grad_proj_hbm, tap_hbm, res_hbm,
    line_ref, tap_ref, res_ref, sem,
):
    sub = lax.broadcasted_iota(jnp.int32, (SUB, LANES), 0)
    for n in range(rim_ref.shape[2] // LANES):
        at = lanes_of(n)
        for i in range(3):
            behind = rim_ref[i, :, at].astype(F32)[:SUB]
            value = tail_ref[i, pl.ds(HALO - SUB, SUB), at]
            for j in range(1, span + 1):
                added = spread(taps_ref[i, pl.ds(j, 1), at]) * (mask_ref[j - 1] * behind)
                value = value + pltpu.roll(jnp.where(sub < j, added, 0.0), SUB - j, 0)
            whole = jnp.concatenate([tail_ref[i, pl.ds(0, HALO - SUB), at], value], axis=0)
            line_ref[i, :, at] = whole.astype(BF16)
    copies = [pltpu.make_async_copy(line_ref, grad_proj_hbm.at[:, pl.ds(rows - HALO, HALO), :], sem.at[0])]
    copies[0].start()
    total = total_of(parts_ref[g].astype(F32) for g in range(parts_ref.shape[0]))
    for i in range(3):
        tap_ref[i] = total[i * SUB : i * SUB + tap_ref.shape[1]]
    res_ref[...] = total[3 * SUB :]
    copies.append(pltpu.make_async_copy(tap_ref, tap_hbm, sem.at[1]))
    copies.append(pltpu.make_async_copy(res_ref, res_hbm, sem.at[2]))
    for copy in copies[1:]:
        copy.start()
    for copy in copies:
        copy.wait()


def per_device(projected, short_taps, pole_decay, residues, doc_lengths, cotangent):
    rows, chans = projected.shape[1:]
    taps = short_taps.shape[1]
    span = taps - 1
    modes = pole_decay.shape[0]
    docs = doc_lengths.shape[0]
    shards = lax.axis_size("ctx")
    steps = rows // SUB
    tiles = chans // LANES
    full_steps = steps + span
    pack_shape = (tiles, 2 * steps + 4 * modes, SUB, LANES)
    query_shape = (tiles, steps, SUB, LANES)

    vmem = pl.BlockSpec(memory_space=pltpu.VMEM)
    hbm = pl.BlockSpec(memory_space=pltpu.HBM)
    free = jax.ShapeDtypeStruct
    dma = pltpu.SemaphoreType.DMA

    def in_hbm(*arrays):
        return [pltpu.with_memory_space_constraint(a, pltpu.HBM) for a in arrays]

    def in_vmem(*arrays):
        return [pltpu.with_memory_space_constraint(a, pltpu.VMEM) for a in arrays]

    def call(kernel, name, out_shape, in_specs, scratch, limit, flops, aliases=None):
        return pl.pallas_call(
            kernel,
            out_shape=tuple(space(shape, kind) for shape, kind, space in out_shape),
            in_specs=in_specs,
            out_specs=tuple(hbm if o[2] is pltpu.HBM else vmem for o in out_shape),
            scratch_shapes=scratch,
            input_output_aliases=aliases or {},
            compiler_params=pltpu.CompilerParams(vmem_limit_bytes=limit << 20),
            cost_estimate=pl.CostEstimate(flops=flops, bytes_accessed=4 << 20, transcendentals=0),
            name=name,
        )

    same_scratch = pltpu.VMEM((span, steps, SUB, LANES), F32)
    cum_scratch = pltpu.VMEM((2, steps, SUB, LANES), F32)
    chunk_scratch = pltpu.VMEM((4, full_steps, SUB, LANES), F32)
    coming_scratch = pltpu.VMEM((tiles, 2, modes, LANES), F32)

    left, proj, cot, taps_near, poles, weights, keeps, rim_masks, picks = call(
        functools.partial(load_kernel, steps, span),
        "load",
        [
            ((3, HALO, chans), BF16, free),
            ((tiles, 3, rows, LANES), BF16, pltpu.VMEM),
            ((tiles, rows, LANES), BF16, pltpu.VMEM),
            ((3, taps, chans), F32, pltpu.VMEM),
            ((modes, chans), F32, pltpu.VMEM),
            ((modes, chans), F32, pltpu.VMEM),
            ((full_steps + span, SUB, LANES), F32, pltpu.VMEM),
            ((taps + 1, SUB, LANES), F32, pltpu.VMEM),
            ((2, shards, chans // 2), F32, pltpu.VMEM),
        ],
        [hbm] * 6,
        [pltpu.SMEM((docs,), jnp.int32), dma((5,)), dma((tiles, 2))],
        8,
        1_000_000,
    )(*in_hbm(doc_lengths, projected, cotangent, short_taps, pole_decay, residues))
    left = shift(left, 1)

    edges, rims, tokens = call(
        functools.partial(edges_kernel, steps, span, modes),
        "edges",
        [
            ((2, modes, chans), F32, pltpu.VMEM),
            ((tiles, 4, SUB, LANES), F32, pltpu.VMEM),
            ((tiles, rows, 4 * LANES), BF16, pltpu.VMEM),
        ],
        [vmem] * 5,
        [
            same_scratch,
            pltpu.VMEM((2, steps, SUB, LANES), F32),
            pltpu.VMEM((4, steps, SUB, LANES), F32),
            pltpu.VMEM((2, steps, SUB, LANES), F32),
        ],
        12,
        40_000_000,
    )(*in_vmem(proj, cot, taps_near, poles, keeps))

    outgoing, left = call(
        functools.partial(rims_kernel, rows, span, modes),
        "rims",
        [
            ((shards, 2 * modes, chans // 2), BF16, pltpu.VMEM),
            ((3, SUB, chans), F32, pltpu.VMEM),
        ],
        [vmem] * 6,
        [
            pltpu.VMEM((3, 2 * SUB, LANES), F32),
            pltpu.VMEM((tiles, 2, SUB, LANES), F32),
            pltpu.VMEM((2, modes, chans), F32),
        ],
        8,
        1_000_000,
    )(*in_vmem(edges, rims, taps_near, poles, rim_masks), left)

    states = lax.all_to_all(outgoing, "ctx", split_axis=0, concat_axis=0, tiled=True)

    feats, res_sums, pack_first, pack, query = call(
        functools.partial(local_kernel, steps, span, modes),
        "local",
        [
            ((tiles, 2, steps, SUB, LANES), F32, pltpu.VMEM),
            ((2, modes, chans), F32, pltpu.VMEM),
            (pack_shape[1:], F32, pltpu.VMEM),
            (pack_shape, F32, pltpu.HBM),
            (query_shape, F32, pltpu.HBM),
        ],
        [vmem] * 6,
        [
            same_scratch,
            chunk_scratch,
            pltpu.VMEM((modes, LANES), F32),
            pltpu.VMEM(pack_shape, F32),
            pltpu.VMEM(query_shape, F32),
            dma((tiles, 2)),
        ],
        16,
        60_000_000,
    )(*in_vmem(tokens, left, taps_near, poles, weights, keeps))

    sums, ahead = call(
        functools.partial(sums_kernel, rows, steps, span, modes),
        "sums",
        [((SUM_ROWS, chans), BF16, free), ((3, HALO, chans), BF16, free)],
        [vmem] * 9 + [hbm],
        [
            pltpu.VMEM(pack_shape, F32),
            same_scratch,
            cum_scratch,
            chunk_scratch,
            coming_scratch,
            pltpu.VMEM((3, steps, SUB, LANES), F32),
            pltpu.VMEM((3 * SUB * SUB, chans), F32),
            pltpu.VMEM((3, HALO, chans), F32),
            dma((tiles,)),
        ],
        12,
        30_000_000,
    )(
        *in_vmem(tokens, left, poles, keeps, picks),
        states,
        *in_vmem(feats, res_sums, pack_first),
        *in_hbm(pack),
    )

    behind = shift(ahead, -1)

    near = 4
    far = shards // near

    def around(block, hop):
        return lax.ppermute(
            block, "ctx", [(i, i // near * near + (i + hop) % near) for i in range(shards)]
        )

    (parts,) = call(
        spread_kernel, "spread", [((far, SUM_ROWS, chans), BF16, pltpu.VMEM)], [vmem] * 4, [], 4, 100_000
    )(*(around(sums, hop) for hop in (1, 2, 3)), sums)
    groups = [[f * near + n for f in range(far)] for n in range(near)]
    gathered = lax.all_to_all(parts, "ctx", 0, 0, tiled=True, axis_index_groups=groups)
    gated, grad_proj, tail, tail_mask = call(
        functools.partial(outputs_kernel, rows, steps, span, modes),
        "outputs",
        [
            ((rows, chans), BF16, pltpu.HBM),
            ((3, rows, chans), BF16, pltpu.HBM),
            ((3, HALO, chans), F32, pltpu.VMEM),
            ((span, SUB, LANES), F32, pltpu.VMEM),
        ],
        [vmem] * 8 + [hbm] * 2,
        [
            pltpu.VMEM(pack_shape, F32),
            pltpu.VMEM(query_shape, F32),
            pltpu.VMEM((span, full_steps, SUB, LANES), F32),
            cum_scratch,
            pltpu.VMEM((1, full_steps, SUB, LANES), F32),
            coming_scratch,
            pltpu.VMEM((3, full_steps, SUB, LANES), F32),
            pltpu.VMEM((4, steps, SUB, LANES), F32),
            pltpu.VMEM((tiles, rows, LANES), BF16),
            pltpu.VMEM((tiles, 3, rows, LANES), BF16),
            dma((tiles,)),
            dma((tiles,)),
            dma((tiles, 2)),
        ],
        16,
        40_000_000,
    )(
        *in_vmem(tokens, taps_near, poles, keeps, picks),
        states,
        *in_vmem(feats, pack_first),
        *in_hbm(pack, query),
    )
    grad_proj, grad_tap, grad_res = call(
        functools.partial(final_kernel, rows, span),
        "final",
        [
            ((3, rows, chans), BF16, pltpu.HBM),
            ((3, taps, chans), F32, pltpu.HBM),
            ((modes, chans), F32, pltpu.HBM),
        ],
        [hbm] + [vmem] * 5,
        [
            pltpu.VMEM((3, HALO, chans), BF16),
            pltpu.VMEM((3, taps, chans), F32),
            pltpu.VMEM((modes, chans), F32),
            dma((3,)),
        ],
        4,
        500_000,
        aliases={0: 0},
    )(*in_hbm(grad_proj), gathered, *in_vmem(tail), behind, *in_vmem(taps_near, tail_mask))
    return (gated, grad_proj, grad_tap, grad_res)


def solution(mesh):
    placed = (
        P(None, "ctx", "tp"),
        P(None, None, "tp"),
        P(None, "tp"),
        P(None, "tp"),
        P(),
        P("ctx", "tp"),
    )
    return jax.shard_map(
        per_device,
        mesh=mesh,
        in_specs=placed,
        out_specs=(P("ctx", "tp"), P(None, "ctx", "tp"), P(None, None, "tp"), P(None, "tp")),
        check_vma=False,
    )
```

```python
import functools
import math

import jax
import jax.numpy as jnp
from jax import lax
from jax.experimental import pallas as pl
from jax.experimental.pallas import tpu as pltpu
from jax.sharding import PartitionSpec as P

F32 = jnp.float32
BF16 = jnp.bfloat16
SUB = 8
LANES = 128
HALO = 16
SUM_ROWS = 32
MAX_DOC = 4096


def shift(block, distance):
    count = lax.axis_size("ctx")
    route = [(i, i + distance) for i in range(count) if 0 <= i + distance < count]
    return lax.ppermute(block, "ctx", route)


def spread(line):
    return jnp.broadcast_to(line, (SUB, LANES))


def power(base, exponent):
    for _ in range(int(math.log2(exponent))):
        base = base * base
    return base


def total_of(terms):
    terms = list(terms)
    while len(terms) > 1:
        terms = [a + b for a, b in zip(terms[::2], terms[1::2])] + terms[len(terms) & ~1 :]
    return terms[0]


def doc_ends(lens_ref):
    ends, total = [], jnp.int32(0)
    for d in range(lens_ref.shape[0]):
        total = total + lens_ref[d]
        ends.append(total)
    return ends


def keep_at(token, ends):
    starts = token == 0
    for end in ends:
        starts = jnp.logical_or(starts, token == end)
    return jnp.where(starts, 0.0, 1.0)


def fill_keep(keep_ref, ends, start, steps, span):
    token = lax.broadcasted_iota(jnp.int32, (SUB, LANES), 0) * steps + start
    for r in range(-span, steps + span):
        keep_ref[r + span] = keep_at(token + r, ends)


def fill_same(same_ref, keep_ref, span):
    for r in range(same_ref.shape[1]):
        running = keep_ref[r + span]
        same_ref[0, r] = running
        for j in range(2, span + 1):
            running = running * keep_ref[r + span - j + 1]
            same_ref[j - 1, r] = running


def fill_cum(cum_ref, keep_ref, steps, span):
    running = jnp.ones((SUB, LANES), F32)
    for r in range(steps):
        running = running * keep_ref[r + span]
        cum_ref[0, r] = running
    running = jnp.ones((SUB, LANES), F32)
    for r in range(steps - 1, -1, -1):
        running = running * keep_ref[r + 1 + span]
        cum_ref[1, r] = running


def fill_pick(pick_ref, ends, start, rows):
    shards = pick_ref.shape[1]
    last_start, next_start = jnp.int32(0), jnp.int32(shards * rows)
    for end in ends:
        last_start = jnp.where(end < start, jnp.maximum(last_start, end), last_start)
        next_start = jnp.where(end > start + rows, jnp.minimum(next_start, end), next_start)
    owner = lax.broadcasted_iota(jnp.int32, pick_ref.shape[1:], 0) * rows
    pick_ref[0] = jnp.where(owner + rows > last_start, 1.0, 0.0)
    pick_ref[1] = jnp.where(owner < next_start, 1.0, 0.0)


def fill_rim_masks(mask_ref, ends, start, rows, span):
    last_start, next_start = jnp.int32(0), jnp.int32(1 << 30)
    for end in ends:
        last_start = jnp.where(end < start + rows, jnp.maximum(last_start, end), last_start)
        next_start = jnp.where(end > start, jnp.minimum(next_start, end), next_start)
    sub = lax.broadcasted_iota(jnp.int32, (SUB, LANES), 0)
    token = start + sub
    running = jnp.ones((SUB, LANES), F32)
    for j in range(span):
        running = running * keep_at(token - j, ends)
        mask_ref[j] = running
    mask_ref[span] = jnp.where(jnp.logical_and(sub < span, token >= last_start), 1.0, 0.0)
    mask_ref[span + 1] = jnp.where(jnp.logical_and(sub < span, token < next_start), 1.0, 0.0)


def at_step(r):
    return pl.ds(r * SUB, SUB)


def lanes_of(i):
    return pl.ds(i * LANES, LANES)


def load_kernel(
    steps, span,
    lens_hbm, proj_hbm, cot_hbm, taps_hbm, pole_hbm, res_hbm,
    left_ref, proj_ref, cot_ref, taps_ref, pole_ref, res_ref, keep_ref, rim_mask_ref, pick_ref,
    lens_ref, small_sem, tile_sem,
):
    tiles, _, rows, _ = proj_ref.shape
    lens_copy = pltpu.make_async_copy(lens_hbm, lens_ref, small_sem.at[0])
    copies = [
        pltpu.make_async_copy(proj_hbm.at[:, pl.ds(rows - HALO, HALO), :], left_ref, small_sem.at[4]),
        pltpu.make_async_copy(taps_hbm, taps_ref, small_sem.at[1]),
        pltpu.make_async_copy(pole_hbm, pole_ref, small_sem.at[2]),
        pltpu.make_async_copy(res_hbm, res_ref, small_sem.at[3]),
    ]
    for n in range(tiles):
        at = lanes_of(n)
        copies.append(pltpu.make_async_copy(proj_hbm.at[:, :, at], proj_ref.at[n], tile_sem.at[n, 0]))
        copies.append(pltpu.make_async_copy(cot_hbm.at[:, at], cot_ref.at[n], tile_sem.at[n, 1]))
    lens_copy.start()
    for copy in copies:
        copy.start()
    lens_copy.wait()
    start = lax.axis_index("ctx") * rows
    ends = doc_ends(lens_ref)
    fill_keep(keep_ref, ends, start, steps, span)
    fill_rim_masks(rim_mask_ref, ends, start, rows, span)
    fill_pick(pick_ref, ends, start, rows)
    for copy in copies:
        copy.wait()


def fir_steps(span, first, last, value_at, same_ref, taps):
    windows = [[value_at(i, first - 1 - j) for j in range(span)] for i in range(len(taps))]
    for r in range(first, last):
        same = [same_ref[j - 1, r] for j in range(1, span + 1)]
        results = []
        for i, stream_taps in enumerate(taps):
            windows[i] = [value_at(i, r)] + windows[i][:span]
            terms = [stream_taps[j] * (same[j - 1] * windows[i][j]) for j in range(1, span + 1)]
            results.append(total_of([stream_taps[0] * windows[i][0]] + terms))
        yield r, results


def fill_chunks(chunk_ref, tokens_ref, n, left_ref, streams, steps, span):
    sub = lax.broadcasted_iota(jnp.int32, (SUB, LANES), 0)
    lane_at = pl.ds(pl.multiple_of(n * LANES, LANES), LANES)
    for place, i in enumerate(streams):
        values = []
        for r in range(0, steps, 2):
            pair = tokens_ref[n, pl.ds(r * SUB, 2 * SUB), lanes_of(i)].astype(F32)
            values += [pair[:SUB], pair[SUB:]]
        for r in range(steps):
            chunk_ref[place, r + span] = values[r]
        for r in range(span if i < 3 else 0):
            halo = spread(left_ref[i, pl.ds(SUB - span + r, 1), lane_at])
            chunk_ref[place, r] = jnp.where(sub == 0, halo, pltpu.roll(values[steps - span + r], 1, 0))


def edges_kernel(
    steps, span, modes,
    proj_ref, cot_ref, taps_ref, pole_ref, keep_ref,
    edge_ref, rim_ref, tokens_ref,
    same_ref, mask_ref, chunk_ref, feat_ref,
):
    tiles, _, rows, _ = proj_ref.shape
    fill_same(same_ref, keep_ref, span)
    sub = lax.broadcasted_iota(jnp.int32, (SUB, LANES), 0)
    running = jnp.ones((SUB, LANES), F32)
    ahead = jnp.where(sub == 0, 0.0, 1.0)
    for r in range(steps - 1, -1, -1):
        mask_ref[0, r] = running if r >= span else ahead * running
        running = running * keep_ref[r + span]
    through = [running]
    running = jnp.ones((SUB, LANES), F32)
    for r in range(steps):
        mask_ref[1, r] = running if r >= span else ahead * running
        running = running * keep_ref[r + 1 + span]
    through.append(running)

    def tile_step(n, carry):
        for i in range(4):
            natural = (proj_ref[n, i] if i < 3 else cot_ref[n]).astype(F32)
            rim_ref[n, i] = natural[:SUB]
            ordered = jnp.swapaxes(natural.reshape(SUB, steps, LANES), 0, 1)
            chunk_ref[i] = ordered
            tokens_ref[n, :, lanes_of(i)] = ordered.reshape(rows, LANES).astype(BF16)

        def chunk(i, r):
            value = chunk_ref[i, r % steps]
            return value if r >= 0 else pltpu.roll(value, 1, 0)

        lane_at = pl.ds(pl.multiple_of(n * LANES, LANES), LANES)
        taps = [[spread(taps_ref[i, pl.ds(j, 1), lane_at]) for j in range(span + 1)] for i in range(3)]
        for r, (query, key, value) in fir_steps(span, 0, steps, chunk, same_ref, taps):
            feat_ref[0, r] = key * value * mask_ref[0, r]
            feat_ref[1, r] = query * chunk(3, r) * mask_ref[1, r]

        poles = [spread(pole_ref[pl.ds(m, 1), lane_at]) for m in range(modes)]
        for way in range(2):
            state = [jnp.zeros((SUB, LANES), F32)] * modes
            for r in range(steps) if way == 0 else range(steps - 1, -1, -1):
                source = feat_ref[way, r]
                state = [poles[m] * state[m] + source for m in range(modes)]
            open_ = through[way]
            factors = [power(poles[m], steps) for m in range(modes)]
            for hop in (1, 2, 4):
                move = hop if way == 0 else SUB - hop
                for m in range(modes):
                    state[m] = state[m] + (factors[m] * open_) * pltpu.roll(state[m], move, 0)
                    factors[m] = factors[m] * factors[m]
                open_ = open_ * pltpu.roll(open_, move, 0)
            last = SUB - 1 if way == 0 else 0
            for m in range(modes):
                edge_ref[way, pl.ds(m, 1), lane_at] = state[m][last : last + 1]
        return carry

    lax.fori_loop(0, tiles, tile_step, 0, unroll=True)


def rims_kernel(
    rows, span, modes,
    edge_ref, rim_ref, taps_ref, pole_ref, mask_ref, left_ref,
    send_ref, left_out_ref,
    ext_ref, line_ref, out_ref,
):
    tiles = rim_ref.shape[0]
    for n in range(tiles):
        at = lanes_of(n)
        made = []
        for i in range(3):
            left_out_ref[i, :, at] = left_ref[i, :, at].astype(F32)[HALO - SUB :]
            ext_ref[i, pl.ds(0, SUB)] = left_out_ref[i, :, at]
            ext_ref[i, pl.ds(SUB, SUB)] = rim_ref[n, i]
            value = spread(taps_ref[i, pl.ds(0, 1), at]) * rim_ref[n, i]
            for j in range(1, span + 1):
                value = value + spread(taps_ref[i, pl.ds(j, 1), at]) * (mask_ref[j - 1] * ext_ref[i, pl.ds(SUB - j, SUB)])
            made.append(value)
        line_ref[n, 0] = made[1] * made[2] * mask_ref[span]
        line_ref[n, 1] = made[0] * rim_ref[n, 3] * mask_ref[span + 1]
        pole = pole_ref[:, at]
        scale, bit, left_over = jnp.ones((modes, LANES), F32), pole, rows - span
        while left_over:
            if left_over & 1:
                scale = scale * bit
            bit = bit * bit
            left_over >>= 1
        for way in range(2):
            running = jnp.zeros((modes, LANES), F32)
            for t in range(span) if way == 0 else range(span - 1, -1, -1):
                running = running * pole + spread(line_ref[n, way, pl.ds(t, 1), :])
            out_ref[way, :, at] = edge_ref[way, :, at] + (scale * running if way == 0 else running)
    half = out_ref.shape[2] // 2
    ahead, behind = (
        jnp.concatenate([out_ref[way, :, pl.ds(0, half)], out_ref[way, :, pl.ds(half, half)]], axis=0).astype(BF16)
        for way in range(2)
    )
    me = lax.axis_index("ctx")

    def fill(value):
        def one(d, carry):
            send_ref[d] = value
            return carry

        return one

    lax.fori_loop(0, me, fill(behind), 0)
    lax.fori_loop(me, send_ref.shape[0], fill(ahead), 0)


def local_kernel(
    steps, span, modes,
    tokens_ref, left_ref, taps_ref, pole_ref, res_ref, keep_ref,
    feat_ref, sums_ref, pack_first_ref, pack_hbm, query_hbm,
    same_ref, chunk_ref, coef_ref, pack_ref, query_ref, out_sem,
):
    tiles = tokens_ref.shape[0]
    fill_same(same_ref, keep_ref, span)
    sub = lax.broadcasted_iota(jnp.int32, (SUB, LANES), 0)

    def run(first, count):
        running = keep_ref[first + span]
        for r in range(first + 1, first + count):
            running = running * keep_ref[r + span]
        return running

    through = [run(0, steps), run(1, steps)]
    onward = keep_ref[steps + span]

    def tile_results(n):
        return (
            pltpu.make_async_copy(pack_ref.at[n], pack_hbm.at[n], out_sem.at[n, 0]),
            pltpu.make_async_copy(query_ref.at[n], query_hbm.at[n], out_sem.at[n, 1]),
        )

    def tile_step(n, carry):
        lane_at = pl.ds(pl.multiple_of(n * LANES, LANES), LANES)
        fill_chunks(chunk_ref, tokens_ref, n, left_ref, range(4), steps, span)

        def chunk(i, r):
            return chunk_ref[i, r + span]

        taps = [[spread(taps_ref[i, pl.ds(j, 1), lane_at]) for j in range(span + 1)] for i in range(3)]
        for r, (query, key, value) in fir_steps(span, 0, steps, chunk, same_ref, taps):
            query_ref[n, r] = query
            feat_ref[n, 0, r] = key
            feat_ref[n, 1, r] = value

        pole_rows = pole_ref[:, lane_at]
        coef_ref[...] = res_ref[:, lane_at] * jnp.sqrt(1.0 - pole_rows * pole_rows)
        poles = [spread(pole_ref[pl.ds(m, 1), lane_at]) for m in range(modes)]
        coefs = [spread(coef_ref[pl.ds(m, 1), :]) for m in range(modes)]
        ends = []
        res_sums = [jnp.zeros((SUB, LANES), F32)] * modes
        for way in range(2):
            state = [jnp.zeros((SUB, LANES), F32)] * modes
            for r in range(steps) if way == 0 else range(steps - 1, -1, -1):
                if way == 0:
                    keep, source = keep_ref[r + span], feat_ref[n, 0, r] * feat_ref[n, 1, r]
                else:
                    keep, source = keep_ref[r + 1 + span], chunk(3, r) * query_ref[n, r]
                state = [(poles[m] * keep) * state[m] + source for m in range(modes)]
                pack_ref[n, way * steps + r] = total_of(coefs[m] * state[m] for m in range(modes))
                if way == 1:
                    carried = feat_ref[n, 0, r] * feat_ref[n, 1, r]
                    res_sums = [res_sums[m] + carried * state[m] for m in range(modes)]
            ends.append(state)

        for way in range(2):
            head = 0 if way == 0 else SUB - 1
            back = 1 if way == 0 else SUB - 1
            for m in range(modes):
                state = ends[way][m]
                factor = power(poles[m], steps)
                open_ = through[way]
                unit = factor * open_
                for hop in (1, 2, 4):
                    move = hop if way == 0 else SUB - hop
                    inside = sub >= hop if way == 0 else sub < SUB - hop
                    far = jnp.where(inside, pltpu.roll(state, move, 0), 0.0)
                    state = state + (factor * open_) * far
                    unit = unit * jnp.where(inside, pltpu.roll(unit, move, 0), 1.0)
                    open_ = open_ * jnp.where(inside, pltpu.roll(open_, move, 0), 1.0)
                    factor = factor * factor
                state = jnp.where(sub == head, 0.0, pltpu.roll(state, back, 0))
                unit = jnp.where(sub == head, 1.0, pltpu.roll(unit, back, 0))
                at = 2 * steps + way * 2 * modes + m
                pack_ref[n, at] = coefs[m] * state
                pack_ref[n, at + modes] = coefs[m] * unit
                if way == 1:
                    seen = poles[m] * onward * ends[0][m]
                    total = jnp.sum(res_sums[m] + seen * state, axis=0, keepdims=True)
                    sums_ref[0, pl.ds(m, 1), lane_at] = total
                    sums_ref[1, pl.ds(m, 1), lane_at] = jnp.sum(seen * unit, axis=0, keepdims=True)
        for copy in tile_results(n):
            copy.start()
        return carry

    lax.fori_loop(0, tiles, tile_step, 0)
    pack_first_ref[...] = pack_ref[0]
    for n in range(tiles):
        for copy in tile_results(n):
            copy.wait()


def fill_coming(coming_ref, states_ref, pick_ref, pole_ref, rows):
    shards = states_ref.shape[0]
    me = lax.axis_index("ctx")
    modes, chans = pole_ref.shape
    full = power(pole_ref[...], rows)
    half = chans // 2
    full = jnp.concatenate([full[:, :half], full[:, half:]], axis=0)
    weight = jnp.ones(full.shape, F32)
    totals = [jnp.zeros(full.shape, F32)] * 2
    for hop in range(1, min(shards - 1, -(-MAX_DOC // rows)) + 1):
        for way, j in enumerate((me - hop, me + hop)):
            inside = jnp.logical_and(j >= 0, j < shards).astype(F32)
            held = jnp.clip(j, 0, shards - 1)
            seen = jnp.broadcast_to(pick_ref[way, pl.ds(held, 1), :], full.shape) * inside
            totals[way] = totals[way] + (weight * seen) * states_ref[held].astype(F32)
        weight = weight * full
    for way, state in enumerate(totals):
        for n in range(chans // LANES):
            top, left = divmod(n * LANES, half)
            coming_ref[n, way] = state[top * modes : (top + 1) * modes, left : left + LANES]


def combine(way, n, steps, modes, pole_ref, pack_ref, coming_ref, cum_ref, lane_at):
    poles = [spread(pole_ref[pl.ds(m, 1), lane_at]) for m in range(modes)]
    at = 2 * steps + way * 2 * modes
    state = [
        pack_ref[n, at + m] + pack_ref[n, at + modes + m] * spread(coming_ref[n, way, pl.ds(m, 1), :])
        for m in range(modes)
    ]
    for r in range(steps) if way == 0 else range(steps - 1, -1, -1):
        state = [poles[m] * state[m] for m in range(modes)]
        yield r, pack_ref[n, way * steps + r] + cum_ref[way, r] * total_of(state)


def sums_kernel(
    rows, steps, span, modes,
    tokens_ref, left_ref, pole_ref, keep_ref, pick_ref, states_ref, feat_ref, res_ref, pack_first_ref, pack_hbm,
    out_hbm, rim_ref,
    pack_ref, same_ref, cum_ref, chunk_ref, coming_ref, grad_ref, sums_ref, line_ref, total_ref, tile_sem, out_sem,
):
    tiles = feat_ref.shape[0]
    shards = states_ref.shape[0]

    def load(n):
        return pltpu.make_async_copy(pack_hbm.at[n], pack_ref.at[n], tile_sem.at[n])

    for n in range(1, tiles):
        load(n).start()
    pack_ref[0] = pack_first_ref[...]
    fill_same(same_ref, keep_ref, span)
    fill_cum(cum_ref, keep_ref, steps, span)
    sums_ref[...] = jnp.zeros_like(sums_ref)
    line_ref[...] = jnp.zeros_like(line_ref)
    fill_coming(coming_ref, states_ref, pick_ref, pole_ref, rows)
    scale = 1.0 / math.sqrt(shards * rows)

    def tile_step(n, carry):
        lane_at = pl.ds(pl.multiple_of(n * LANES, LANES), LANES)
        fill_chunks(chunk_ref, tokens_ref, n, left_ref, range(4), steps, span)

        @pl.when(n > 0)
        def _():
            load(n).wait()

        for way in range(2):
            for r, value in combine(way, n, steps, modes, pole_ref, pack_ref, coming_ref, cum_ref, lane_at):
                if way == 0:
                    grad_ref[0, r] = chunk_ref[3, r + span] * value
                else:
                    grad_ref[1, r] = value * feat_ref[n, 1, r]
                    grad_ref[2, r] = value * feat_ref[n, 0, r]
        for i in range(3):
            for r in range(span):
                line_ref[i, pl.ds(r, 1), lane_at] = grad_ref[i, r, pl.ds(0, 1), :]
        tap_sums = [[jnp.zeros((SUB, LANES), F32)] * (span + 1)] * 3
        windows = [[chunk_ref[i, span - 1 - j] for j in range(span)] for i in range(3)]
        for r in range(steps):
            same = [same_ref[j - 1, r] for j in range(1, span + 1)]
            for i in range(3):
                here = grad_ref[i, r]
                windows[i] = [chunk_ref[i, r + span]] + windows[i][:span]
                masked = [here] + [same[j] * here for j in range(span)]
                tap_sums[i] = [tap_sums[i][j] + masked[j] * windows[i][j] for j in range(span + 1)]
        for i in range(3):
            for j in range(span + 1):
                sums_ref[pl.ds((i * SUB + j) * SUB, SUB), lane_at] = tap_sums[i][j]
        return carry

    lax.fori_loop(0, tiles, tile_step, 0)
    rim_ref[...] = line_ref[...].astype(BF16)
    shape = (3 * SUB, 3 * SUB * SUB)
    at = lax.broadcasted_iota(jnp.int32, shape, 0)
    col = lax.broadcasted_iota(jnp.int32, shape, 1)
    gather = jnp.where((col >> 3) == at, 1.0, 0.0).astype(BF16)
    high = sums_ref[...].astype(BF16)
    low = (sums_ref[...] - high.astype(F32)).astype(BF16)
    taps = jnp.dot(gather, high, preferred_element_type=F32) + jnp.dot(gather, low, preferred_element_type=F32)
    pole = pole_ref[...]
    back = jnp.concatenate([coming_ref[n, 1] for n in range(tiles)], axis=1)
    res = (res_ref[0] + res_ref[1] * back) * jnp.sqrt(1.0 - pole * pole)
    total_ref[...] = (jnp.concatenate([taps, res], axis=0) * scale).astype(BF16)
    copies = [pltpu.make_async_copy(total_ref, out_hbm.at[g], out_sem.at[g]) for g in range(out_hbm.shape[0])]
    for copy in copies:
        copy.start()
    for copy in copies:
        copy.wait()


def outputs_kernel(
    rows, steps, span, modes,
    tokens_ref, taps_ref, pole_ref, keep_ref, pick_ref, states_ref, feat_ref, pack_first_ref,
    pack_hbm, query_hbm,
    gated_hbm, grad_proj_hbm, tail_ref, tail_mask_ref,
    pack_ref, query_ref, same_ref, cum_ref, chunk_ref, coming_ref, grad_ref, out_ref, gated_ref, grad_proj_ref,
    pack_sem, query_sem, out_sem,
):
    tiles = feat_ref.shape[0]

    def load_pack(n):
        return pltpu.make_async_copy(pack_hbm.at[n], pack_ref.at[n], pack_sem.at[n])

    def load_query(n):
        return pltpu.make_async_copy(query_hbm.at[n], query_ref.at[n], query_sem.at[n])

    def results(n):
        at = pl.ds(n * LANES, LANES)
        if not isinstance(n, int):
            at = pl.ds(pl.multiple_of(n * LANES, LANES), LANES)
        return (
            pltpu.make_async_copy(gated_ref.at[n], gated_hbm.at[:, at], out_sem.at[n, 0]),
            pltpu.make_async_copy(grad_proj_ref.at[n], grad_proj_hbm.at[:, :, at], out_sem.at[n, 1]),
        )

    for n in range(tiles):
        load_query(n).start()
        if n > 0:
            load_pack(n).start()
    pack_ref[0] = pack_first_ref[...]
    fill_same(same_ref, keep_ref, span)
    fill_cum(cum_ref, keep_ref, steps, span)
    sub = lax.broadcasted_iota(jnp.int32, (SUB, LANES), 0)
    fill_coming(coming_ref, states_ref, pick_ref, pole_ref, rows)

    def tile_step(n, carry):
        lane_at = pl.ds(pl.multiple_of(n * LANES, LANES), LANES)
        fill_chunks(chunk_ref, tokens_ref, n, None, (3,), steps, span)

        @pl.when(n > 0)
        def _():
            load_pack(n).wait()

        for way in range(2):
            for r, value in combine(way, n, steps, modes, pole_ref, pack_ref, coming_ref, cum_ref, lane_at):
                if way == 0:
                    grad_ref[0, r] = chunk_ref[0, r + span] * value
                    out_ref[3, r] = value
                else:
                    grad_ref[1, r] = value * feat_ref[n, 1, r]
                    grad_ref[2, r] = value * feat_ref[n, 0, r]
        for i in range(3):
            for r in range(span):
                grad_ref[i, steps + r] = jnp.where(sub == SUB - 1, 0.0, pltpu.roll(grad_ref[i, r], SUB - 1, 0))
        taps = [[spread(taps_ref[i, pl.ds(j, 1), lane_at]) for j in range(span + 1)] for i in range(3)]
        windows = [[grad_ref[i, r] for r in range(span)] for i in range(3)]
        for r in range(steps):
            same = [same_ref[j - 1, r + j] for j in range(1, span + 1)]
            for i in range(3):
                windows[i] = windows[i][-span:] + [grad_ref[i, r + span]]
                terms = [taps[i][j] * (same[j - 1] * windows[i][j]) for j in range(1, span + 1)]
                out_ref[i, r] = total_of([taps[i][0] * windows[i][0]] + terms)
        gated_copy, grad_copy = results(n)
        for i in range(3):
            natural = jnp.swapaxes(out_ref[i], 0, 1).reshape(SUB * steps, LANES)
            tail_ref[i, :, lane_at] = natural[SUB * steps - HALO :]
            grad_proj_ref[n, i] = natural.astype(BF16)
        grad_copy.start()
        load_query(n).wait()
        gated_ref[n] = jnp.swapaxes(query_ref[n] * out_ref[3], 0, 1).reshape(SUB * steps, LANES).astype(BF16)
        gated_copy.start()
        return carry

    lax.fori_loop(0, tiles, tile_step, 0)
    for n in range(tiles):
        for copy in results(n):
            copy.wait()
    for j in range(1, span + 1):
        for r in range(span):
            tail_mask_ref[j - 1, pl.ds(r, 1), :] = same_ref[j - 1, steps + r, pl.ds(SUB - 1, 1), :]


def far_kernel(parts_ref, after_ref, out_ref):
    del after_ref
    out_ref[...] = total_of(parts_ref[g].astype(F32) for g in range(parts_ref.shape[0])).astype(BF16)


def final_kernel(
    rows, span, partial_hbm, own_ref, one_ref, two_ref, three_ref, tail_ref, rim_ref, taps_ref, mask_ref,
    grad_proj_hbm, tap_hbm, res_hbm,
    line_ref, tap_ref, res_ref, sem,
):
    sub = lax.broadcasted_iota(jnp.int32, (SUB, LANES), 0)
    for n in range(rim_ref.shape[2] // LANES):
        at = lanes_of(n)
        for i in range(3):
            behind = rim_ref[i, :, at].astype(F32)[:SUB]
            value = tail_ref[i, pl.ds(HALO - SUB, SUB), at]
            for j in range(1, span + 1):
                added = spread(taps_ref[i, pl.ds(j, 1), at]) * (mask_ref[j - 1] * behind)
                value = value + pltpu.roll(jnp.where(sub < j, added, 0.0), SUB - j, 0)
            whole = jnp.concatenate([tail_ref[i, pl.ds(0, HALO - SUB), at], value], axis=0)
            line_ref[i, :, at] = whole.astype(BF16)
    copies = [pltpu.make_async_copy(line_ref, grad_proj_hbm.at[:, pl.ds(rows - HALO, HALO), :], sem.at[0])]
    copies[0].start()
    own, one, two, three = (ref[...].astype(F32) for ref in (own_ref, one_ref, two_ref, three_ref))
    total = (own + two) + (one + three)
    for i in range(3):
        tap_ref[i] = total[i * SUB : i * SUB + tap_ref.shape[1]]
    res_ref[...] = total[3 * SUB :]
    copies.append(pltpu.make_async_copy(tap_ref, tap_hbm, sem.at[1]))
    copies.append(pltpu.make_async_copy(res_ref, res_hbm, sem.at[2]))
    for copy in copies[1:]:
        copy.start()
    for copy in copies:
        copy.wait()


def per_device(projected, short_taps, pole_decay, residues, doc_lengths, cotangent):
    rows, chans = projected.shape[1:]
    taps = short_taps.shape[1]
    span = taps - 1
    modes = pole_decay.shape[0]
    docs = doc_lengths.shape[0]
    shards = lax.axis_size("ctx")
    steps = rows // SUB
    tiles = chans // LANES
    full_steps = steps + span
    near = 4
    far = shards // near
    pack_shape = (tiles, 2 * steps + 4 * modes, SUB, LANES)
    query_shape = (tiles, steps, SUB, LANES)

    vmem = pl.BlockSpec(memory_space=pltpu.VMEM)
    hbm = pl.BlockSpec(memory_space=pltpu.HBM)
    free = jax.ShapeDtypeStruct
    dma = pltpu.SemaphoreType.DMA

    def in_hbm(*arrays):
        return [pltpu.with_memory_space_constraint(a, pltpu.HBM) for a in arrays]

    def in_vmem(*arrays):
        return [pltpu.with_memory_space_constraint(a, pltpu.VMEM) for a in arrays]

    def call(kernel, name, out_shape, in_specs, scratch, limit, flops, aliases=None):
        return pl.pallas_call(
            kernel,
            out_shape=tuple(space(shape, kind) for shape, kind, space in out_shape),
            in_specs=in_specs,
            out_specs=tuple(hbm if o[2] is pltpu.HBM else vmem for o in out_shape),
            scratch_shapes=scratch,
            input_output_aliases=aliases or {},
            compiler_params=pltpu.CompilerParams(vmem_limit_bytes=limit << 20),
            cost_estimate=pl.CostEstimate(flops=flops, bytes_accessed=4 << 20, transcendentals=0),
            name=name,
        )

    same_scratch = pltpu.VMEM((span, steps, SUB, LANES), F32)
    cum_scratch = pltpu.VMEM((2, steps, SUB, LANES), F32)
    chunk_scratch = pltpu.VMEM((4, full_steps, SUB, LANES), F32)
    coming_scratch = pltpu.VMEM((tiles, 2, modes, LANES), F32)

    left, proj, cot, taps_near, poles, weights, keeps, rim_masks, picks = call(
        functools.partial(load_kernel, steps, span),
        "load",
        [
            ((3, HALO, chans), BF16, free),
            ((tiles, 3, rows, LANES), BF16, pltpu.VMEM),
            ((tiles, rows, LANES), BF16, pltpu.VMEM),
            ((3, taps, chans), F32, pltpu.VMEM),
            ((modes, chans), F32, pltpu.VMEM),
            ((modes, chans), F32, pltpu.VMEM),
            ((full_steps + span, SUB, LANES), F32, pltpu.VMEM),
            ((taps + 1, SUB, LANES), F32, pltpu.VMEM),
            ((2, shards, chans // 2), F32, pltpu.VMEM),
        ],
        [hbm] * 6,
        [pltpu.SMEM((docs,), jnp.int32), dma((5,)), dma((tiles, 2))],
        8,
        1_000_000,
    )(*in_hbm(doc_lengths, projected, cotangent, short_taps, pole_decay, residues))
    left = shift(left, 1)

    edges, rims, tokens = call(
        functools.partial(edges_kernel, steps, span, modes),
        "edges",
        [
            ((2, modes, chans), F32, pltpu.VMEM),
            ((tiles, 4, SUB, LANES), F32, pltpu.VMEM),
            ((tiles, rows, 4 * LANES), BF16, pltpu.VMEM),
        ],
        [vmem] * 5,
        [
            same_scratch,
            pltpu.VMEM((2, steps, SUB, LANES), F32),
            pltpu.VMEM((4, steps, SUB, LANES), F32),
            pltpu.VMEM((2, steps, SUB, LANES), F32),
        ],
        12,
        40_000_000,
    )(*in_vmem(proj, cot, taps_near, poles, keeps))

    outgoing, left = call(
        functools.partial(rims_kernel, rows, span, modes),
        "rims",
        [
            ((shards, 2 * modes, chans // 2), BF16, pltpu.VMEM),
            ((3, SUB, chans), F32, pltpu.VMEM),
        ],
        [vmem] * 6,
        [
            pltpu.VMEM((3, 2 * SUB, LANES), F32),
            pltpu.VMEM((tiles, 2, SUB, LANES), F32),
            pltpu.VMEM((2, modes, chans), F32),
        ],
        8,
        1_000_000,
    )(*in_vmem(edges, rims, taps_near, poles, rim_masks), left)

    states = lax.all_to_all(outgoing, "ctx", split_axis=0, concat_axis=0, tiled=True)

    feats, res_sums, pack_first, pack, query = call(
        functools.partial(local_kernel, steps, span, modes),
        "local",
        [
            ((tiles, 2, steps, SUB, LANES), F32, pltpu.VMEM),
            ((2, modes, chans), F32, pltpu.VMEM),
            (pack_shape[1:], F32, pltpu.VMEM),
            (pack_shape, F32, pltpu.HBM),
            (query_shape, F32, pltpu.HBM),
        ],
        [vmem] * 6,
        [
            same_scratch,
            chunk_scratch,
            pltpu.VMEM((modes, LANES), F32),
            pltpu.VMEM(pack_shape, F32),
            pltpu.VMEM(query_shape, F32),
            dma((tiles, 2)),
        ],
        16,
        60_000_000,
    )(*in_vmem(tokens, left, taps_near, poles, weights, keeps))

    sums, ahead = call(
        functools.partial(sums_kernel, rows, steps, span, modes),
        "sums",
        [((far, SUM_ROWS, chans), BF16, pltpu.HBM), ((3, HALO, chans), BF16, free)],
        [vmem] * 9 + [hbm],
        [
            pltpu.VMEM(pack_shape, F32),
            same_scratch,
            cum_scratch,
            chunk_scratch,
            coming_scratch,
            pltpu.VMEM((3, steps, SUB, LANES), F32),
            pltpu.VMEM((3 * SUB * SUB, chans), F32),
            pltpu.VMEM((3, HALO, chans), F32),
            pltpu.VMEM((SUM_ROWS, chans), BF16),
            dma((tiles,)),
            dma((far,)),
        ],
        12,
        30_000_000,
    )(
        *in_vmem(tokens, left, poles, keeps, picks),
        states,
        *in_vmem(feats, res_sums, pack_first),
        *in_hbm(pack),
    )

    behind = shift(ahead, -1)


    def around(block, hop):
        return lax.ppermute(
            block, "ctx", [(i, i // near * near + (i + hop) % near) for i in range(shards)]
        )

    groups = [[f * near + n for f in range(far)] for n in range(near)]
    gathered = lax.all_to_all(sums, "ctx", 0, 0, tiled=True, axis_index_groups=groups)
    gated, grad_proj, tail, tail_mask = call(
        functools.partial(outputs_kernel, rows, steps, span, modes),
        "outputs",
        [
            ((rows, chans), BF16, pltpu.HBM),
            ((3, rows, chans), BF16, pltpu.HBM),
            ((3, HALO, chans), F32, pltpu.VMEM),
            ((span, SUB, LANES), F32, pltpu.VMEM),
        ],
        [vmem] * 8 + [hbm] * 2,
        [
            pltpu.VMEM(pack_shape, F32),
            pltpu.VMEM(query_shape, F32),
            pltpu.VMEM((span, full_steps, SUB, LANES), F32),
            cum_scratch,
            pltpu.VMEM((1, full_steps, SUB, LANES), F32),
            coming_scratch,
            pltpu.VMEM((3, full_steps, SUB, LANES), F32),
            pltpu.VMEM((4, steps, SUB, LANES), F32),
            pltpu.VMEM((tiles, rows, LANES), BF16),
            pltpu.VMEM((tiles, 3, rows, LANES), BF16),
            dma((tiles,)),
            dma((tiles,)),
            dma((tiles, 2)),
        ],
        16,
        40_000_000,
    )(
        *in_vmem(tokens, taps_near, poles, keeps, picks),
        states,
        *in_vmem(feats, pack_first),
        *in_hbm(pack, query),
    )
    (sums,) = call(far_kernel, "far", [((SUM_ROWS, chans), BF16, free)], [vmem] * 2, [], 4, 100_000)(
        gathered, *in_vmem(tail_mask)
    )
    near_sums = [sums] + [around(sums, hop) for hop in (1, 2, 3)]

    grad_proj, grad_tap, grad_res = call(
        functools.partial(final_kernel, rows, span),
        "final",
        [
            ((3, rows, chans), BF16, pltpu.HBM),
            ((3, taps, chans), F32, pltpu.HBM),
            ((modes, chans), F32, pltpu.HBM),
        ],
        [hbm] + [vmem] * 8,
        [
            pltpu.VMEM((3, HALO, chans), BF16),
            pltpu.VMEM((3, taps, chans), F32),
            pltpu.VMEM((modes, chans), F32),
            dma((3,)),
        ],
        4,
        500_000,
        aliases={0: 0},
    )(*in_hbm(grad_proj), *near_sums, *in_vmem(tail), behind, *in_vmem(taps_near, tail_mask))
    return (gated, grad_proj, grad_tap, grad_res)


def solution(mesh):
    placed = (
        P(None, "ctx", "tp"),
        P(None, None, "tp"),
        P(None, "tp"),
        P(None, "tp"),
        P(),
        P("ctx", "tp"),
    )
    return jax.shard_map(
        per_device,
        mesh=mesh,
        in_specs=placed,
        out_specs=(P("ctx", "tp"), P(None, "ctx", "tp"), P(None, None, "tp"), P(None, "tp")),
        check_vma=False,
    )
```
